128 devices in a mesh: row: 8 (over y, core), col: 16 (over z, x).
Axes of the slice: x: 4, y: 4, z: 4, core: 2. Of those that a mesh axis runs over, the one named last changes fastest.
Arguments:
- a_blocks: bfloat16 [8, 512, 64, 1728], P('row', 'col'), may hold values from -0.75 to 0.75
- a_cols: int32 [8, 512, 27], P('row', 'col'), may hold values from 0 to 47
- p_blocks: bfloat16 [8, 64, 32768], P('row', None, 'col'), may hold values from -2.09375 to 2.09375
- contrib_peer: int32 [8, 13824], P('row', 'col'), may hold values from 0 to 15
- contrib_slot: int32 [8, 13824], P('row', 'col'), may hold values from 0 to 53
- outbound_term_lists: int32 [8, 256, 13], P('row', 'col'), may hold values from 0 to 863, as said below
- send_count: int32 [8, 256], P('row', 'col'), may hold values from 0 to 13, as said below
- keep: int32 [8], replicated, may hold values from 0 to 1, as said below
Outputs:
- coarse: float32 [8, 64, 55296], P('row', None, 'col')
The draws below stay inside these ranges and needn't reach their ends.
Inputs may be any that keep to these rules, and one draw needn't show every extreme that they name: keep[r] + keep[r2] = 1 for rows r and r2 half the row axis apart. `send_count`: a device's count for its own column is 0; in each row of devices one column gets exactly 13 terms from every other device of that row. `outbound_term_lists`: entries 0 to send_count[p] - 1 of list p of a device name, each once, exactly its terms e with contrib_peer[e] = p; later entries are arbitrary; every term whose contrib_peer differs from the device's column is listed.
All inputs are finite; a program needn't handle non-finite values.
Results may differ from the reference program's by a relative error of at most 0.0041.
Values may be sent and summed in bfloat16 or wider, within the bound.
A program may use at most 192 MiB of HBM per device.

```python
import jax
import jax.numpy as jnp
from jax import lax

B = 64
KA = 27
FB = 32
H = 8
ITEMS = 864
CAP = 13
CS = 54
N_ROW = 8
N_COL = 16


def fine_routes(key):
    heavy_key, count_key, order_key, filler_key = jax.random.split(jax.random.fold_in(key, 17), 4)
    heavy = jax.random.randint(heavy_key, (N_ROW,), 0, N_COL)
    send_counts = jax.random.randint(count_key, (N_ROW, N_COL, N_COL), CAP // 8, 3 * CAP // 4 + 1)
    peer_range = jnp.arange(N_COL, dtype=jnp.int32)
    send_counts = jnp.where(peer_range[None, None, :] == heavy[:, None, None], CAP, send_counts)
    send_counts = jnp.where(peer_range[None, None, :] == peer_range[None, :, None], 0, send_counts)
    order_keys = jax.random.split(order_key, N_ROW * N_COL)
    shuffled = jax.vmap(lambda subkey: jax.random.permutation(subkey, ITEMS))(order_keys).reshape(N_ROW, N_COL, ITEMS)
    list_ends = jnp.cumsum(send_counts, axis=-1)
    term_list_offsets = list_ends - send_counts
    slot_range = jnp.arange(CAP, dtype=jnp.int32)
    position = jnp.minimum(term_list_offsets[..., None] + slot_range, ITEMS - 1)
    active_term_mask = slot_range < send_counts[..., None]
    filler = jax.random.randint(filler_key, (N_ROW, N_COL, N_COL, CAP), 0, ITEMS)
    listed_items = jnp.take_along_axis(shuffled, position.reshape(N_ROW, N_COL, N_COL * CAP), axis=-1)
    listed_items = jnp.where(active_term_mask, listed_items.reshape(N_ROW, N_COL, N_COL, CAP), filler)
    ranks = jnp.arange(ITEMS, dtype=jnp.int32)
    rank_owner = jnp.sum((ranks[None, None, :, None] >= list_ends[:, :, None, :]).astype(jnp.int32), axis=-1)
    remote_total = list_ends[..., -1]
    own_cols = jnp.broadcast_to(peer_range[None, :, None], (N_ROW, N_COL, ITEMS))
    rank_owner = jnp.where(ranks[None, None, :] < remote_total[..., None], rank_owner, own_cols)
    owners = jax.vmap(lambda order_row, owner_row: jnp.zeros((ITEMS,), jnp.int32).at[order_row].set(owner_row))(shuffled.reshape(-1, ITEMS), rank_owner.reshape(-1, ITEMS))
    return (send_counts, listed_items, owners.reshape(N_ROW, N_COL, ITEMS))


def draw_contrib_peer(key, part):
    send_counts, listed_items, owners = fine_routes(key)
    return owners.reshape(N_ROW, N_COL * ITEMS).astype(jnp.int32)


def draw_outbound_term_lists(key, part):
    send_counts, listed_items, owners = fine_routes(key)
    return listed_items.reshape(N_ROW, N_COL * N_COL, CAP).astype(jnp.int32)


def draw_send_count(key, part):
    send_counts, listed_items, owners = fine_routes(key)
    return send_counts.reshape(N_ROW, N_COL * N_COL).astype(jnp.int32)


def draw_keep(key, part):
    lower_half = jax.random.randint(jax.random.fold_in(key, 5), (N_ROW // 2,), 0, 2)
    return jnp.concatenate([lower_half, 1 - lower_half]).astype(jnp.int32)


def plant(result, own_key, least, high):
    extent = result.shape
    index_at = [jax.random.randint(jax.random.fold_in(own_key, axis), (), 0, extent[axis]) for axis in range(len(extent))]
    result = result.at[tuple(index_at)].set(least)
    longest = extent.index(max(extent))
    index_at[longest] = (index_at[longest] + 1) % extent[longest]
    return result.at[tuple(index_at)].set(high)


def levels(rng, extent, shards, smallest, largest):
    gain = 1.0
    for axis_at, blocks in shards:
        steps = jax.random.uniform(jax.random.fold_in(jax.random.fold_in(rng, 6), axis_at), (blocks,), jnp.float32, smallest / len(shards), largest / len(shards))
        gain = gain * jnp.repeat(jnp.exp(steps), extent[axis_at] // blocks).reshape((-1,) + (1,) * (len(extent) - 1 - axis_at))
    return gain


def noise(key, shape, spread, most, cuts=(), kind=jnp.bfloat16):
    array = spread * jax.random.normal(key, shape, jnp.float32)
    if cuts:
        array = array * levels(key, shape, cuts, -0.22, 0.18)
    return jnp.clip(array, -most, most).astype(kind)


def setup_inputs(seed: int = 0) -> dict:
    arg_keys = jax.random.split(jax.random.key(seed), 9)
    a_blocks = noise(arg_keys[0], (N_ROW, N_COL * FB, B, KA * B), B ** -0.5, 0.75, ((0, 8), (1, 16)))
    a_cols = plant(jax.random.randint(arg_keys[1], (N_ROW, N_COL * FB, KA), 0, FB + 2 * H), jax.random.fold_in(arg_keys[1], 1), 0, (FB + 2 * H) - 1).astype(jnp.int32)
    p_blocks = noise(arg_keys[2], (N_ROW, B, N_COL * FB * B), 0.35, 2.09375, ((0, 8), (2, 16)))
    contrib_peer = draw_contrib_peer(jax.random.fold_in(arg_keys[8], 71), 0)
    contrib_slot = plant(jax.random.randint(arg_keys[4], (N_ROW, N_COL * ITEMS), 0, CS), jax.random.fold_in(arg_keys[4], 1), 0, CS - 1).astype(jnp.int32)
    outbound_term_lists = draw_outbound_term_lists(jax.random.fold_in(arg_keys[8], 71), 0)
    send_count = draw_send_count(jax.random.fold_in(arg_keys[8], 71), 0)
    keep = draw_keep(jax.random.fold_in(arg_keys[8], 71), 0)
    return {"a_blocks": a_blocks, "a_cols": a_cols, "p_blocks": p_blocks, "contrib_peer": contrib_peer, "contrib_slot": contrib_slot, "outbound_term_lists": outbound_term_lists, "send_count": send_count, "keep": keep}


def reference(a_blocks, a_cols, p_blocks, contrib_peer, contrib_slot, outbound_term_lists, send_count, keep):
    prolong = p_blocks.reshape(N_ROW, B, N_COL * FB, B).transpose(0, 2, 1, 3)
    padded = jnp.pad(prolong, ((0, 0), (H, H), (0, 0), (0, 0)))
    pieces = jnp.arange(N_COL * CAP, dtype=jnp.int32)

    def device_step(accumulated, index):
        row_index = (index // N_COL).astype(jnp.int32)
        col_index = (index % N_COL).astype(jnp.int32)
        zero = jnp.zeros((), jnp.int32)
        rim_table = lax.dynamic_slice(padded, (row_index, col_index * FB, zero, zero), (1, FB + 2 * H, B, B))[0]
        rows_a = lax.dynamic_slice(a_blocks, (row_index, col_index * FB, zero, zero), (1, FB, B, KA * B))[0]
        a_split = rows_a.reshape(FB, B, KA, B).transpose(0, 2, 1, 3)
        block_cols = lax.dynamic_slice(a_cols, (row_index, col_index * FB, zero), (1, FB, KA))[0]
        picked = rim_table[block_cols]
        product = jnp.einsum("ikab,ikbc->ikac", a_split.astype(jnp.float32), picked.astype(jnp.float32)).astype(jnp.bfloat16)
        prolong_own = lax.dynamic_slice(prolong, (row_index, col_index * FB, zero, zero), (1, FB, B, B))[0]
        galerkin = jnp.einsum("iba,ikbc->ikac", prolong_own.astype(jnp.float32), product.astype(jnp.float32))
        galerkin = galerkin.astype(jnp.bfloat16).reshape(ITEMS, B, B).astype(jnp.float32)
        owner_cols = lax.dynamic_slice(contrib_peer, (row_index, col_index * ITEMS), (1, ITEMS))[0]
        slot_ids = lax.dynamic_slice(contrib_slot, (row_index, col_index * ITEMS), (1, ITEMS))[0]
        local_weight = jnp.where(owner_cols == col_index, jnp.float32(1.0), jnp.float32(0.0))
        accumulated = accumulated.at[row_index, col_index, slot_ids].add(galerkin * local_weight[:, None, None])
        listed_items = lax.dynamic_slice(outbound_term_lists, (row_index, col_index * N_COL, zero), (1, N_COL, CAP))[0].reshape(-1)
        row_term_count = lax.dynamic_slice(send_count, (row_index, col_index * N_COL), (1, N_COL))[0]
        active_term_mask = (pieces % CAP) < row_term_count[pieces // CAP]
        moved = galerkin[listed_items] * jnp.where(active_term_mask, jnp.float32(1.0), jnp.float32(0.0))[:, None, None]
        accumulated = accumulated.at[row_index, pieces // CAP, slot_ids[listed_items]].add(moved)
        return accumulated, None

    accumulated = jnp.zeros((N_ROW, N_COL, CS, B, B), jnp.float32)
    accumulated, _ = lax.scan(device_step, accumulated, jnp.arange(N_ROW * N_COL, dtype=jnp.int32))
    partner = jnp.roll(accumulated, N_ROW // 2, axis=0)
    keep_weight = jnp.where(keep == 1, jnp.float32(1.0), jnp.float32(0.0))[:, None, None, None, None]
    coarse = (accumulated + partner) * keep_weight
    return coarse.transpose(0, 3, 1, 2, 4).reshape(N_ROW, B, N_COL * CS * B)
```

```python
import functools

import jax
import jax.numpy as jnp
from jax import lax
from jax.experimental import pallas as pl
from jax.experimental.pallas import tpu as pltpu
from jax.sharding import PartitionSpec as P

B = 64
KA = 27
FB = 32
H = 8
CAP = 13
CS = 54
N_COL = 16
KP = 14
GROUP = 4

F32 = jnp.float32
BF16 = jnp.bfloat16
VM = pltpu.VMEM
SM = pltpu.SMEM


def left_half(shape):
    return lax.broadcasted_iota(jnp.int32, shape, len(shape) - 1) < B


def q_kernel(p_ref, a_ref, q_ref):
    for ii in range(GROUP):
        p = p_ref[:, ii * B : (ii + 1) * B]
        q = lax.dot_general(p, a_ref[ii], (((0,), (0,)), ((), ())), preferred_element_type=F32)
        q_ref[ii, :, : KA * B] = q.astype(BF16)
        q_ref[ii, :, KA * B :] = jnp.zeros((B, B), BF16)


def fill_table(table_ref, pieces):
    at = 0
    for ref, tiles in pieces:
        for m in range(tiles):
            tile = ref[:, m * 2 * B : (m + 1) * 2 * B].astype(F32)
            turned = pltpu.roll(tile, B, 1)
            low = left_half(tile.shape)
            table_ref[at] = jnp.where(low, tile, turned).astype(BF16)
            table_ref[at + 1] = jnp.where(low, turned, tile).astype(BF16)
            at += 2


def packed(pair):
    return jnp.where(left_half((B // 2, 2 * B)), pair[: B // 2], pair[B // 2 :])


def listed_kernel(items, counts, slots, cols, q_ref, p_ref, left_ref, right_ref, out_ref, table_ref, slot_ref):
    fill_table(table_ref, ((left_ref, H // 2), (p_ref, FB // 2), (right_ref, H // 2)))
    zero = jnp.zeros((B, 2 * B), BF16)

    @pl.loop(0, N_COL)
    def _(p):
        for j in range(CAP):
            e = items[p, j]
            live = j < counts[p]
            i = e // KA
            k = e - i * KA
            kp = k // 2
            odd = (k - 2 * kp) == 1
            tile = q_ref[i, :, pl.ds(pl.multiple_of(kp * 2 * B, 2 * B), 2 * B)]
            t = table_ref[cols[i, k]]
            rhs = jnp.concatenate([jnp.where(odd, zero, t), jnp.where(odd, t, zero)], axis=0)
            g = jnp.dot(tile, rhs, preferred_element_type=F32)
            out_ref[p, j] = packed(g).astype(BF16)
            slot_ref[p, j] = jnp.where(live, slots[i, k], CS)


def local_kernel(slots, cols, q_ref, table_ref, even_ref, odd_ref):
    even_ref[...] = jnp.zeros_like(even_ref)
    odd_ref[...] = jnp.zeros_like(odd_ref)
    zero = jnp.zeros((B, 2 * B), BF16)

    @pl.loop(0, FB)
    def _(i):
        for kp in range(KP):
            tile = q_ref[i, :, kp * 2 * B : (kp + 1) * 2 * B]
            k0 = 2 * kp
            k1 = 2 * kp + 1
            t0 = table_ref[cols[i, k0]]
            if k1 < KA:
                t1 = table_ref[cols[i, k1]]
                rhs = jnp.concatenate(
                    [jnp.concatenate([t0, zero], axis=1), jnp.concatenate([zero, t1], axis=1)], axis=0
                )
            else:
                rhs = jnp.concatenate([t0, zero], axis=0)
            g = jnp.dot(tile, rhs, preferred_element_type=F32)
            even_ref[slots[i, k0]] += packed(g[:, : 2 * B])
            if k1 < KA:
                odd_ref[slots[i, k1]] += packed(g[:, 2 * B :])


def merge_kernel(slots, even_ref, odd_ref, arrived_ref, acc_ref, sent_ref, work):
    work[...] = even_ref[...]

    @pl.loop(0, N_COL)
    def _(p):
        for j in range(CAP):
            work[slots[p, j]] += arrived_ref[p, j].astype(F32)

    @pl.loop(0, CS)
    def _(s):
        total = work[s] + odd_ref[s]
        acc_ref[s] = total
        sent_ref[s] = total.astype(BF16)


def final_kernel(keep, acc_ref, partner_ref, out_ref):
    weight = keep[0].astype(F32)
    low = left_half((B // 2, 2 * B))
    for m in range(CS // 2):
        a = (acc_ref[2 * m] + partner_ref[2 * m].astype(F32)) * weight
        b = (acc_ref[2 * m + 1] + partner_ref[2 * m + 1].astype(F32)) * weight
        lanes = slice(m * 2 * B, (m + 1) * 2 * B)
        out_ref[0, : B // 2, lanes] = jnp.where(low, a, pltpu.roll(b, B, 1))
        out_ref[0, B // 2 :, lanes] = jnp.where(low, pltpu.roll(a, B, 1), b)


def params(mib):
    return pltpu.CompilerParams(vmem_limit_bytes=mib * 2**20)


def specs(*spaces):
    return [pl.BlockSpec(memory_space=s) for s in spaces]


def on_device(
    a_blocks, a_cols, p_blocks, contrib_peer, contrib_slot, outbound_term_lists, send_count, keep
):
    rows = lax.axis_size("row")
    columns = lax.axis_size("col")
    own_row = lax.axis_index("row")
    own_col = lax.axis_index("col")
    prolong = p_blocks[0]
    ends = columns - 1
    left = lax.ppermute(prolong[:, -H * B :], "col", [(i, i + 1) for i in range(ends)])
    right = lax.ppermute(prolong[:, : H * B], "col", [(i + 1, i) for i in range(ends)])
    q = pl.pallas_call(
        q_kernel,
        grid=(FB // GROUP,),
        in_specs=[
            pl.BlockSpec((B, GROUP * B), lambda g: (0, g)),
            pl.BlockSpec((GROUP, B, KA * B), lambda g: (g, 0, 0)),
        ],
        out_specs=pl.BlockSpec((GROUP, B, KP * 2 * B), lambda g: (g, 0, 0)),
        out_shape=jax.ShapeDtypeStruct((FB, B, KP * 2 * B), BF16),
        compiler_params=params(24),
        cost_estimate=pl.CostEstimate(flops=10**9, bytes_accessed=15 * 10**6, transcendentals=0),
        name="q_stage",
    )(prolong, a_blocks[0])
    cols = a_cols[0]
    slots = contrib_slot.reshape(FB, KA)
    peers = contrib_peer.reshape(FB, KA)
    outgoing, table, out_slots = pl.pallas_call(
        listed_kernel,
        in_specs=specs(SM, SM, SM, SM, VM, VM, VM, VM),
        out_specs=specs(VM, VM, SM),
        out_shape=[
            jax.ShapeDtypeStruct((N_COL, CAP, B // 2, 2 * B), BF16),
            jax.ShapeDtypeStruct((FB + 2 * H, B, 2 * B), BF16),
            jax.ShapeDtypeStruct((N_COL, CAP), jnp.int32),
        ],
        compiler_params=params(32),
        name="listed_stage",
    )(outbound_term_lists[0], send_count[0], slots, cols, q, prolong, left, right)
    arrived = lax.all_to_all(outgoing, "col", split_axis=0, concat_axis=0, tiled=True)
    arrived_slots = lax.all_to_all(out_slots, "col", split_axis=0, concat_axis=0, tiled=True)
    local_slots = jnp.where(peers == own_col, slots, CS)
    even, odd = pl.pallas_call(
        local_kernel,
        in_specs=specs(SM, SM, VM, VM),
        out_specs=specs(VM, VM),
        out_shape=[jax.ShapeDtypeStruct((CS + 1, B // 2, 2 * B), F32)] * 2,
        compiler_params=params(32),
        cost_estimate=pl.CostEstimate(flops=2 * 10**10, bytes_accessed=15 * 10**6, transcendentals=0),
        name="local_stage",
    )(local_slots, cols, q, table)
    total, sent = pl.pallas_call(
        merge_kernel,
        in_specs=specs(SM, VM, VM, VM),
        out_specs=specs(VM, VM),
        out_shape=[
            jax.ShapeDtypeStruct((CS, B // 2, 2 * B), F32),
            jax.ShapeDtypeStruct((CS, B // 2, 2 * B), BF16),
        ],
        scratch_shapes=[pltpu.VMEM((CS + 1, B // 2, 2 * B), F32)],
        compiler_params=params(32),
        name="merge_stage",
    )(arrived_slots, even, odd, arrived)
    half = rows // 2
    partner = lax.ppermute(sent, "row", [(i, (i + half) % rows) for i in range(rows)])
    return pl.pallas_call(
        final_kernel,
        in_specs=specs(SM, VM, VM),
        out_specs=pl.BlockSpec(memory_space=VM),
        out_shape=jax.ShapeDtypeStruct((1, B, CS * B), F32),
        compiler_params=params(32),
        name="final_stage",
    )(lax.dynamic_slice(keep, (own_row,), (1,)), total, partner)


def solution(mesh):
    placed = (
        P("row", "col", None, None),
        P("row", "col", None),
        P("row", None, "col"),
        P("row", "col"),
        P("row", "col"),
        P("row", "col", None),
        P("row", "col"),
        P(),
    )
    return jax.shard_map(
        on_device, mesh=mesh, in_specs=placed, out_specs=P("row", None, "col"), check_vma=False
    )
```

```python
import jax
import jax.numpy as jnp
from jax import lax
from jax.experimental import pallas as pl
from jax.experimental.pallas import tpu as pltpu
from jax.sharding import PartitionSpec as P

B = 64
KA = 27
FB = 32
H = 8
ITEMS = 864
CAP = 13
CS = 54
N_ROW = 8
N_COL = 16
SIDE = 4
KP = 14
W = 2 * B
RR = B // 2
SP = 64
NONE = 63
GROUP = 4
CHUNK_TILES = (0, 8, 14, 21, 27)
CHUNKS = 4
SEND_ROWS = 27 * 16
PER = RR // CHUNKS

F32 = jnp.float32
BF16 = jnp.bfloat16
MESH = pl.DeviceIdType.MESH


def iota(shape, dim):
    return lax.broadcasted_iota(jnp.int32, shape, dim)


def packed(pair):
    return jnp.where(iota((RR, W), 1) < B, pair[:RR], pair[RR:])


def fill_table(table_ref, at, tiles, load):
    for m in range(tiles):
        tile = load(m).astype(F32)
        turned = pltpu.roll(tile, B, 1)
        low = iota(tile.shape, 1) < B
        table_ref[at + 2 * m] = jnp.where(low, tile, turned).astype(BF16)
        table_ref[at + 2 * m + 1] = jnp.where(low, turned, tile).astype(BF16)


def kernel(
    cols,
    items,
    counts,
    slot_scalars,
    keep,
    slot_row,
    peer_row,
    p_ref,
    a_ref,
    out_ref,
    a_buf,
    q_buf,
    table,
    halo_left,
    halo_right,
    stage,
    outgoing,
    arrived,
    terms,
    acc,
    own_hot,
    slot_rows,
    y_out,
    y_in,
    a_sems,
    halo_send,
    halo_recv,
    sends,
    recvs,
    y_send,
    y_recv,
):
    row = lax.axis_index("row")
    col = lax.axis_index("col")
    z = col // SIDE
    x = col % SIDE
    partner = ((row + N_ROW // 2) % N_ROW, col)
    before = (row, (col + N_COL - 1) % N_COL)
    after = (row, (col + 1) % N_COL)

    def a_copy(g):
        part = pl.ds(g * GROUP, GROUP)
        return pltpu.make_async_copy(a_ref.at[0, part], a_buf.at[part], a_sems.at[g])

    @pl.loop(0, FB // GROUP)
    def _(g):
        a_copy(g).start()

    barrier = pltpu.get_barrier_semaphore()

    @pl.loop(1, N_COL)
    def _(d):
        pl.semaphore_signal(
            barrier, inc=1, device_id=(row, (col + d) % N_COL), device_id_type=MESH
        )

    pl.semaphore_signal(barrier, inc=1, device_id=partner, device_id_type=MESH)

    fill_table(table, H, FB // 2, lambda m: p_ref[0, :, m * W : (m + 1) * W])
    own_slots = jnp.where(peer_row[...] == col, slot_row[...], NONE)
    own_hot[...] = jnp.where(own_slots == iota((SP, ITEMS), 0), 1.0, 0.0).astype(BF16)
    arrived[col] = jnp.zeros((SEND_ROWS, W), BF16)

    @pl.loop(0, FB // GROUP)
    def _(g):
        a_copy(g).wait()
        for m in range(GROUP // 2):
            pair = p_ref[0, :, pl.ds(pl.multiple_of((g * (GROUP // 2) + m) * W, W), W)]
            for h in range(2):
                i = g * GROUP + 2 * m + h
                q = lax.dot_general(
                    pair[:, h * B : (h + 1) * B],
                    a_buf[i],
                    (((0,), (0,)), ((), ())),
                    preferred_element_type=F32,
                )
                q = q.astype(BF16)
                for kp in range(KP - 1):
                    q_buf[i * KP + kp] = q[:, kp * W : (kp + 1) * W]
                q_buf[i * KP + KP - 1, :, :B] = q[:, (KP - 1) * W :]
                q_buf[i * KP + KP - 1, :, B:] = jnp.zeros((B, B), BF16)

    pl.semaphore_wait(barrier, N_COL)
    to_after = pltpu.make_async_remote_copy(
        src_ref=p_ref.at[0, :, pl.ds((FB - H) * B, H * B)],
        dst_ref=halo_left,
        send_sem=halo_send.at[0],
        recv_sem=halo_recv.at[0],
        device_id=after,
        device_id_type=MESH,
    )
    to_before = pltpu.make_async_remote_copy(
        src_ref=p_ref.at[0, :, pl.ds(0, H * B)],
        dst_ref=halo_right,
        send_sem=halo_send.at[1],
        recv_sem=halo_recv.at[1],
        device_id=before,
        device_id_type=MESH,
    )
    to_after.start()
    to_before.start()
    to_after.wait()
    to_before.wait()
    has_left = jnp.where(col > 0, 1.0, 0.0).astype(F32)
    has_right = jnp.where(col < N_COL - 1, 1.0, 0.0).astype(F32)
    fill_table(
        table, 0, H // 2, lambda m: halo_left[:, m * W : (m + 1) * W].astype(F32) * has_left
    )
    fill_table(
        table, H + FB, H // 2, lambda m: halo_right[:, m * W : (m + 1) * W].astype(F32) * has_right
    )

    zero = jnp.zeros((B, W), BF16)

    def peer_of(n):
        dz = (2 + n // SIDE) % SIDE
        dx = (2 + n % SIDE) % SIDE
        return ((z + dz) % SIDE) * SIDE + (x + dx) % SIDE

    def source_of(n):
        dz = (2 + n // SIDE) % SIDE
        dx = (2 + n % SIDE) % SIDE
        return ((z + SIDE - dz) % SIDE) * SIDE + (x + SIDE - dx) % SIDE

    def send_copy(chunk, n):
        first, last = CHUNK_TILES[chunk], CHUNK_TILES[chunk + 1]
        part = pl.ds(first * 16, (last - first) * 16)
        peer = peer_of(n)
        return pltpu.make_async_remote_copy(
            src_ref=outgoing.at[peer, part],
            dst_ref=arrived.at[col, part],
            send_sem=sends.at[chunk, n],
            recv_sem=recvs.at[chunk, n],
            device_id=(row, peer),
            device_id_type=MESH,
        )

    def recv_copy(chunk, n):
        first, last = CHUNK_TILES[chunk], CHUNK_TILES[chunk + 1]
        part = pl.ds(first * 16, (last - first) * 16)
        peer = source_of(n)
        return pltpu.make_async_remote_copy(
            src_ref=outgoing.at[peer, part],
            dst_ref=arrived.at[peer, part],
            send_sem=sends.at[chunk, n],
            recv_sem=recvs.at[chunk, n],
            device_id=(row, peer),
            device_id_type=MESH,
        )

    place = (iota((16, W), 0) * 16 + iota((16, W), 1) % 16) % CAP

    def list_terms(n):
        p = peer_of(n)
        tags = jnp.full((16, W), NONE, jnp.int32)
        for j in range(CAP):
            e = items[0, p, j]
            i = e // KA
            k = e - i * KA
            kp = k // 2
            odd = (k - 2 * kp) == 1
            tile = q_buf[i * KP + kp]
            t = table[cols[0, i, k]]
            rhs = jnp.concatenate([jnp.where(odd, zero, t), jnp.where(odd, t, zero)], axis=0)
            g = jnp.dot(tile, rhs, preferred_element_type=F32)
            stage[pl.ds(j, RR, stride=CAP), :] = packed(g)
            slot = jnp.where(j < counts[0, p], slot_scalars[0, e], NONE)
            tags = jnp.where(place == j, slot, tags)
        outgoing[p, pl.ds(0, 16)] = tags.astype(F32).astype(BF16)
        outgoing[p, pl.ds(16, RR * CAP)] = stage[...].astype(BF16)
        send_copy(0, n).start()

    pl.loop(0, 10)(list_terms)
    pl.loop(11, N_COL)(list_terms)
    for chunk in range(1, CHUNKS):
        for span in ((0, 10), (11, N_COL)):

            @pl.loop(*span)
            def _(n):
                send_copy(chunk, n).start()

    @pl.loop(0, FB)
    def _(i):
        for kp in range(KP):
            tile = q_buf[i * KP + kp]
            t0 = table[cols[0, i, 2 * kp]]
            if 2 * kp + 1 < KA:
                t1 = table[cols[0, i, 2 * kp + 1]]
                rhs = jnp.concatenate(
                    [jnp.concatenate([t0, zero], axis=1), jnp.concatenate([zero, t1], axis=1)],
                    axis=0,
                )
            else:
                rhs = jnp.concatenate([t0, zero], axis=0)
            g = jnp.dot(tile, rhs, preferred_element_type=F32)
            terms[pl.ds(i * KA + 2 * kp, RR, stride=ITEMS), :] = packed(g[:, :W])
            if 2 * kp + 1 < KA:
                terms[pl.ds(i * KA + 2 * kp + 1, RR, stride=ITEMS), :] = packed(g[:, W:])

    @pl.loop(0, RR)
    def _(r):
        values = terms[pl.ds(pl.multiple_of(r * ITEMS, 8), ITEMS), :].astype(BF16)
        acc[pl.ds(pl.multiple_of(r * SP, SP), SP), :] = jnp.dot(
            own_hot[...], values, preferred_element_type=F32
        )

    lane = iota((1, 2 * W), 1)

    def y_copy(chunk):
        part = pl.ds(chunk * PER * SP, PER * SP)
        return pltpu.make_async_remote_copy(
            src_ref=y_out.at[part],
            dst_ref=y_in.at[part],
            send_sem=y_send.at[chunk],
            recv_sem=y_recv.at[chunk],
            device_id=partner,
            device_id_type=MESH,
        )

    def merge(chunk):
        for span in ((0, 10), (11, N_COL)):

            @pl.loop(*span)
            def _(n):
                recv_copy(chunk, n).wait_recv()

        if chunk == 0:
            group = iota((16, W), 1) // 16
            for half in range(2):
                rows = jnp.full((16, W), float(NONE), F32)
                for s in range(8):
                    src = half * 8 + s
                    tags = arrived[src, 0:16, :].astype(F32)
                    mine = jnp.logical_and(group == s, src != col)
                    rows = jnp.where(mine, tags, rows)
                slot_rows[:, half * W : (half + 1) * W] = rows
        for tile in range(CHUNK_TILES[chunk], CHUNK_TILES[chunk + 1]):
            if tile == 0:
                continue
            tau = tile - 1
            first = tau * 16 // CAP
            last = (tau * 16 + 15) // CAP
            slots = slot_rows[tau % CAP : tau % CAP + 1, :]
            r_of = (tau * 16 + lane % 16) // CAP
            values = arrived[:, tile * 16 : tile * 16 + 16, :].reshape(2 * W, W)
            for r in range(first, last + 1):
                hot = jnp.where(r_of == r, slots, -1.0)
                hot = (hot == iota((SP, 2 * W), 0).astype(F32)).astype(F32).astype(BF16)
                acc[r * SP : (r + 1) * SP, :] += jnp.dot(
                    hot, values, preferred_element_type=F32
                )
        part = slice(chunk * PER * SP, (chunk + 1) * PER * SP)
        y_out[part, :] = acc[part, :].astype(BF16)
        y_copy(chunk).start()

    weight = keep[row].astype(F32)

    def finish(chunk):
        y_copy(chunk).wait_recv()
        part = slice(chunk * PER * SP, (chunk + 1) * PER * SP)
        acc[part, :] = (acc[part, :] + y_in[part, :].astype(F32)) * weight
        low = iota((PER, W), 1) < B
        at = chunk * PER
        for m in range(CS // 2):
            a = acc[pl.ds(at * SP + 2 * m, PER, stride=SP), :]
            b = acc[pl.ds(at * SP + 2 * m + 1, PER, stride=SP), :]
            lanes = slice(m * W, (m + 1) * W)
            out_ref[0, at : at + PER, lanes] = jnp.where(low, a, pltpu.roll(b, B, 1))
            out_ref[0, RR + at : RR + at + PER, lanes] = jnp.where(low, pltpu.roll(a, B, 1), b)

    for chunk in range(CHUNKS):
        merge(chunk)
        if chunk > 0:
            finish(chunk - 1)
    finish(CHUNKS - 1)
    for chunk in range(CHUNKS):
        y_copy(chunk).wait_send()
        for span in ((0, 10), (11, N_COL)):

            @pl.loop(*span)
            def _(n):
                send_copy(chunk, n).wait_send()


def on_device(
    a_blocks, a_cols, p_blocks, contrib_peer, contrib_slot, outbound_term_lists, send_count, keep
):
    smem = pl.BlockSpec(memory_space=pltpu.SMEM)
    vmem = pl.BlockSpec(memory_space=pltpu.VMEM)
    dma = pltpu.SemaphoreType.DMA
    return pl.pallas_call(
        kernel,
        in_specs=[smem] * 5 + [vmem] * 3 + [pl.BlockSpec(memory_space=pl.ANY)],
        out_specs=vmem,
        out_shape=jax.ShapeDtypeStruct((1, B, CS * B), F32),
        scratch_shapes=[
            pltpu.VMEM((FB, B, KA * B), BF16),
            pltpu.VMEM((FB * KP, B, W), BF16),
            pltpu.VMEM((FB + 2 * H, B, W), BF16),
            pltpu.VMEM((B, H * B), BF16),
            pltpu.VMEM((B, H * B), BF16),
            pltpu.VMEM((RR * CAP, W), F32),
            pltpu.VMEM((N_COL, SEND_ROWS, W), BF16),
            pltpu.VMEM((N_COL, SEND_ROWS, W), BF16),
            pltpu.VMEM((RR * ITEMS, W), F32),
            pltpu.VMEM((RR * SP, W), F32),
            pltpu.VMEM((SP, ITEMS), BF16),
            pltpu.VMEM((16, 2 * W), F32),
            pltpu.VMEM((RR * SP, W), BF16),
            pltpu.VMEM((RR * SP, W), BF16),
            dma((FB // GROUP,)),
            dma((2,)),
            dma((2,)),
            dma((CHUNKS, N_COL)),
            dma((CHUNKS, N_COL)),
            dma((CHUNKS,)),
            dma((CHUNKS,)),
        ],
        compiler_params=pltpu.CompilerParams(
            collective_id=0, has_side_effects=True, vmem_limit_bytes=52 * 2**20
        ),
        name="galerkin",
    )(
        a_cols,
        outbound_term_lists,
        send_count,
        contrib_slot,
        keep,
        contrib_slot,
        contrib_peer,
        p_blocks,
        a_blocks,
    )


def solution(mesh):
    placed = (
        P("row", "col", None, None),
        P("row", "col", None),
        P("row", None, "col"),
        P("row", "col"),
        P("row", "col"),
        P("row", "col", None),
        P("row", "col"),
        P(),
    )
    return jax.shard_map(
        on_device, mesh=mesh, in_specs=placed, out_specs=P("row", None, "col"), check_vma=False
    )
```

```python
import jax
import jax.numpy as jnp
from jax import lax
from jax.experimental import pallas as pl
from jax.experimental.pallas import tpu as pltpu
from jax.sharding import PartitionSpec as P

B = 64
KA = 27
FB = 32
H = 8
ITEMS = 864
CAP = 13
CS = 54
N_ROW = 8
N_COL = 16
SIDE = 4
KP = 14
W = 2 * B
WW = 4 * B
RR = B // 4
SP = 64
NONE = 63
GROUP = 4
Q_BEFORE = 4
CHUNK_TILES = (0, 5, 8, 11, 14)
CHUNKS = 4
SEND_ROWS = 14 * 16
PER = RR // CHUNKS
Y_ROWS = 2 * PER * CS

F32 = jnp.float32
BF16 = jnp.bfloat16
MESH = pl.DeviceIdType.MESH


def iota(shape, dim):
    return lax.broadcasted_iota(jnp.int32, shape, dim)


def packed(pair):
    return jnp.where(iota((2 * RR, W), 1) < B, pair[: 2 * RR], pair[2 * RR :])


def side_by_side(upper, lower):
    return jnp.concatenate([upper, lower], axis=1)


def fill_table(table_ref, at, tiles, load):
    for m in range(tiles):
        tile = load(m).astype(F32)
        turned = pltpu.roll(tile, B, 1)
        low = iota(tile.shape, 1) < B
        table_ref[at + 2 * m] = jnp.where(low, tile, turned).astype(BF16)
        table_ref[at + 2 * m + 1] = jnp.where(low, turned, tile).astype(BF16)


def kernel(
    cols,
    items,
    counts,
    slot_scalars,
    keep,
    slot_row,
    peer_row,
    p_ref,
    a_ref,
    out_ref,
    a_buf,
    q_buf,
    table,
    halo_left,
    halo_right,
    stage,
    outgoing,
    arrived,
    terms,
    acc,
    own_hot,
    slot_rows,
    y_stage,
    y_out,
    y_in,
    a_sems,
    halo_send,
    halo_recv,
    sends,
    recvs,
    y_send,
    y_recv,
    ready,
):
    row = lax.axis_index("row")
    col = lax.axis_index("col")
    z = col // SIDE
    x = col % SIDE
    partner = ((row + N_ROW // 2) % N_ROW, col)
    before = (row, (col + N_COL - 1) % N_COL)
    after = (row, (col + 1) % N_COL)

    def a_copy(g):
        part = pl.ds(g * GROUP, GROUP)
        return pltpu.make_async_copy(a_ref.at[0, part], a_buf.at[part], a_sems.at[g])

    @pl.loop(0, FB // GROUP)
    def _(g):
        a_copy(g).start()

    barrier = pltpu.get_barrier_semaphore()

    def greet(peer):
        pl.semaphore_signal(barrier, inc=1, device_id=(row, peer), device_id_type=MESH)

    at_edge = jnp.logical_or(x == 0, x == SIDE - 1)

    @pl.when(x == 0)
    def _():
        greet((col + N_COL - 1) % N_COL)

    @pl.when(x == SIDE - 1)
    def _():
        greet((col + 1) % N_COL)

    for d in range(1, SIDE):
        greet(z * SIDE + (x + d) % SIDE)
    for d in range(1, SIDE):
        greet(((z + d) % SIDE) * SIDE + x)
    pl.semaphore_signal(barrier, inc=1, device_id=partner, device_id_type=MESH)

    fill_table(table, H, FB // 2, lambda m: p_ref[0, :, m * W : (m + 1) * W])
    own_slots = jnp.where(peer_row[...] == col, slot_row[...], NONE)
    own_hot[...] = jnp.where(own_slots == iota((SP, ITEMS), 0), 1.0, 0.0).astype(BF16)
    arrived[col] = jnp.zeros((SEND_ROWS, WW), BF16)

    def form_q(g):
        a_copy(g).wait()
        for m in range(GROUP // 2):
            pair = p_ref[0, :, pl.ds(pl.multiple_of((g * (GROUP // 2) + m) * W, W), W)]
            for h in range(2):
                i = g * GROUP + 2 * m + h
                q = lax.dot_general(
                    pair[:, h * B : (h + 1) * B],
                    a_buf[i],
                    (((0,), (0,)), ((), ())),
                    preferred_element_type=F32,
                )
                q = q.astype(BF16)
                for kp in range(KP - 1):
                    q_buf[i * KP + kp] = q[:, kp * W : (kp + 1) * W]
                q_buf[i * KP + KP - 1, :, :B] = q[:, (KP - 1) * W :]
                q_buf[i * KP + KP - 1, :, B:] = jnp.zeros((B, B), BF16)

    pl.loop(0, Q_BEFORE)(form_q)
    pl.semaphore_wait(barrier, 2 * SIDE - 1 + jnp.where(at_edge, 1, 0))
    for d in range(1, SIDE):
        pl.semaphore_signal(
            ready,
            inc=1,
            device_id=(row, ((z + d) % SIDE) * SIDE + x),
            device_id_type=MESH,
        )
    to_after = pltpu.make_async_remote_copy(
        src_ref=p_ref.at[0, :, pl.ds((FB - H) * B, H * B)],
        dst_ref=halo_left,
        send_sem=halo_send.at[0],
        recv_sem=halo_recv.at[0],
        device_id=after,
        device_id_type=MESH,
    )
    to_before = pltpu.make_async_remote_copy(
        src_ref=p_ref.at[0, :, pl.ds(0, H * B)],
        dst_ref=halo_right,
        send_sem=halo_send.at[1],
        recv_sem=halo_recv.at[1],
        device_id=before,
        device_id_type=MESH,
    )
    to_after.start()
    to_before.start()
    pl.loop(Q_BEFORE, FB // GROUP)(form_q)
    to_after.wait()
    to_before.wait()
    pl.semaphore_wait(ready, SIDE - 1)
    has_left = jnp.where(col > 0, 1.0, 0.0).astype(F32)
    has_right = jnp.where(col < N_COL - 1, 1.0, 0.0).astype(F32)
    fill_table(
        table, 0, H // 2, lambda m: halo_left[:, m * W : (m + 1) * W].astype(F32) * has_left
    )
    fill_table(
        table, H + FB, H // 2, lambda m: halo_right[:, m * W : (m + 1) * W].astype(F32) * has_right
    )

    zero = jnp.zeros((B, W), BF16)

    def peer_of(n):
        dz = (2 + n // SIDE) % SIDE
        dx = (2 + n % SIDE) % SIDE
        return ((z + dz) % SIDE) * SIDE + (x + dx) % SIDE

    def source_of(n):
        dz = (2 + n // SIDE) % SIDE
        dx = (2 + n % SIDE) % SIDE
        return ((z + SIDE - dz) % SIDE) * SIDE + (x + SIDE - dx) % SIDE

    def send_copy(chunk, n):
        first, last = CHUNK_TILES[chunk], CHUNK_TILES[chunk + 1]
        part = pl.ds(first * 16, (last - first) * 16)
        peer = peer_of(n)
        return pltpu.make_async_remote_copy(
            src_ref=outgoing.at[peer, part],
            dst_ref=arrived.at[col, part],
            send_sem=sends.at[chunk, n],
            recv_sem=recvs.at[chunk, n],
            device_id=(row, peer),
            device_id_type=MESH,
        )

    def recv_copy(chunk, n):
        first, last = CHUNK_TILES[chunk], CHUNK_TILES[chunk + 1]
        part = pl.ds(first * 16, (last - first) * 16)
        peer = source_of(n)
        return pltpu.make_async_remote_copy(
            src_ref=outgoing.at[peer, part],
            dst_ref=arrived.at[peer, part],
            send_sem=sends.at[chunk, n],
            recv_sem=recvs.at[chunk, n],
            device_id=(row, peer),
            device_id_type=MESH,
        )

    place = (iota((16, WW), 0) * 16 + iota((16, WW), 1) % 16) % CAP

    def list_terms(n):
        p = peer_of(n)
        tags = jnp.full((16, WW), NONE, jnp.int32)
        for j in range(CAP):
            e = items[0, p, j]
            i = e // KA
            k = e - i * KA
            kp = k // 2
            odd = (k - 2 * kp) == 1
            tile = q_buf[i * KP + kp]
            t = table[cols[0, i, k]]
            rhs = jnp.concatenate([jnp.where(odd, zero, t), jnp.where(odd, t, zero)], axis=0)
            g = jnp.dot(tile, rhs, preferred_element_type=F32)
            stage[pl.ds(j, 2 * RR, stride=CAP), :] = packed(g)
            slot = jnp.where(j < counts[0, p], slot_scalars[0, e], NONE)
            tags = jnp.where(place == j, slot, tags)
        outgoing[p, pl.ds(0, 16)] = tags.astype(F32).astype(BF16)
        outgoing[p, pl.ds(16, RR * CAP)] = side_by_side(
            stage[: RR * CAP, :], stage[RR * CAP :, :]
        ).astype(BF16)
        send_copy(0, n).start()

    pl.loop(0, 10)(list_terms)
    pl.loop(11, N_COL)(list_terms)
    for chunk in range(1, CHUNKS):
        for span in ((0, 10), (11, N_COL)):

            @pl.loop(*span)
            def _(n):
                send_copy(chunk, n).start()

    @pl.loop(0, FB)
    def _(i):
        for kp in range(KP):
            tile = q_buf[i * KP + kp]
            t0 = table[cols[0, i, 2 * kp]]
            if 2 * kp + 1 < KA:
                t1 = table[cols[0, i, 2 * kp + 1]]
                rhs = jnp.concatenate(
                    [jnp.concatenate([t0, zero], axis=1), jnp.concatenate([zero, t1], axis=1)],
                    axis=0,
                )
            else:
                rhs = jnp.concatenate([t0, zero], axis=0)
            g = jnp.dot(tile, rhs, preferred_element_type=F32)
            terms[pl.ds(i * KA + 2 * kp, 2 * RR, stride=ITEMS), :] = packed(g[:, :W])
            if 2 * kp + 1 < KA:
                terms[pl.ds(i * KA + 2 * kp + 1, 2 * RR, stride=ITEMS), :] = packed(g[:, W:])

    def own_sum(chunk):
        for r in range(chunk * PER, (chunk + 1) * PER):
            upper = terms[r * ITEMS : (r + 1) * ITEMS, :]
            lower = terms[(RR + r) * ITEMS : (RR + r + 1) * ITEMS, :]
            total = jnp.dot(
                own_hot[...], side_by_side(upper, lower).astype(BF16), preferred_element_type=F32
            )
            acc[r * SP : (r + 1) * SP, :] += total[:, :W]
            acc[(RR + r) * SP : (RR + r + 1) * SP, :] += total[:, W:]

    acc[...] = jnp.zeros_like(acc)

    lane = iota((1, WW), 1)

    def y_copy(chunk):
        part = pl.ds(chunk * Y_ROWS, Y_ROWS)
        return pltpu.make_async_remote_copy(
            src_ref=y_out.at[part],
            dst_ref=y_in.at[part],
            send_sem=y_send.at[chunk],
            recv_sem=y_recv.at[chunk],
            device_id=partner,
            device_id_type=MESH,
        )

    def merge(chunk):
        for span in ((0, 10), (11, N_COL)):

            @pl.loop(*span)
            def _(n):
                recv_copy(chunk, n).wait_recv()

        if chunk == 0:
            group = iota((16, WW), 1) // 16
            rows = jnp.full((16, WW), float(NONE), F32)
            for src in range(N_COL):
                tags = arrived[src, 0:16, :].astype(F32)
                mine = jnp.logical_and(group == src, src != col)
                rows = jnp.where(mine, tags, rows)
            slot_rows[...] = rows
        for tile in range(CHUNK_TILES[chunk], CHUNK_TILES[chunk + 1]):
            if tile == 0:
                continue
            tau = tile - 1
            first = tau * 16 // CAP
            last = (tau * 16 + 15) // CAP
            slots = slot_rows[tau % CAP : tau % CAP + 1, :]
            r_of = (tau * 16 + lane % 16) // CAP
            values = arrived[:, tile * 16 : tile * 16 + 16, :].reshape(WW, WW)
            sub = iota((SP, WW), 0).astype(F32)
            hot = [
                jnp.where(jnp.where(r_of == r, slots, -1.0) == sub, 1.0, 0.0).astype(BF16)
                for r in range(first, last + 1)
            ]
            more = jnp.dot(jnp.concatenate(hot, axis=0), values, preferred_element_type=F32)
            acc[first * SP : (last + 1) * SP, :] += more[:, :W]
            acc[(RR + first) * SP : (RR + last + 1) * SP, :] += more[:, W:]
        for h in range(2):
            for n in range(PER):
                at = (h * RR + chunk * PER + n) * SP
                y_stage[(h * PER + n) * CS : (h * PER + n + 1) * CS, :] = acc[at : at + CS, :]
        y_out[chunk * Y_ROWS : (chunk + 1) * Y_ROWS, :] = y_stage[...].astype(BF16)
        y_copy(chunk).start()

    weight = keep[row].astype(F32)

    def finish(chunk):
        y_copy(chunk).wait_recv()
        y_stage[...] = y_in[chunk * Y_ROWS : (chunk + 1) * Y_ROWS, :].astype(F32)
        for h in range(2):
            for n in range(PER):
                at = (h * RR + chunk * PER + n) * SP
                more = y_stage[(h * PER + n) * CS : (h * PER + n + 1) * CS, :]
                acc[at : at + CS, :] = (acc[at : at + CS, :] + more) * weight
        low = iota((PER, W), 1) < B
        at = chunk * PER
        for m in range(CS // 2):
            lanes = slice(m * W, (m + 1) * W)
            for half in range(2):
                up = half * RR + at
                a = acc[pl.ds(up * SP + 2 * m, PER, stride=SP), :]
                b = acc[pl.ds(up * SP + 2 * m + 1, PER, stride=SP), :]
                out_ref[0, up : up + PER, lanes] = jnp.where(low, a, pltpu.roll(b, B, 1))
                up = 2 * RR + up
                out_ref[0, up : up + PER, lanes] = jnp.where(low, pltpu.roll(a, B, 1), b)

    for chunk in range(CHUNKS):
        own_sum(chunk)
        merge(chunk)
        if chunk > 0:
            finish(chunk - 1)
    finish(CHUNKS - 1)
    for chunk in range(CHUNKS):
        y_copy(chunk).wait_send()
        for span in ((0, 10), (11, N_COL)):

            @pl.loop(*span)
            def _(n):
                send_copy(chunk, n).wait_send()


def on_device(
    a_blocks, a_cols, p_blocks, contrib_peer, contrib_slot, outbound_term_lists, send_count, keep
):
    smem = pl.BlockSpec(memory_space=pltpu.SMEM)
    vmem = pl.BlockSpec(memory_space=pltpu.VMEM)
    dma = pltpu.SemaphoreType.DMA
    return pl.pallas_call(
        kernel,
        in_specs=[smem] * 5 + [vmem] * 3 + [pl.BlockSpec(memory_space=pl.ANY)],
        out_specs=vmem,
        out_shape=jax.ShapeDtypeStruct((1, B, CS * B), F32),
        scratch_shapes=[
            pltpu.VMEM((FB, B, KA * B), BF16),
            pltpu.VMEM((FB * KP, B, W), BF16),
            pltpu.VMEM((FB + 2 * H, B, W), BF16),
            pltpu.VMEM((B, H * B), BF16),
            pltpu.VMEM((B, H * B), BF16),
            pltpu.VMEM((2 * RR * CAP, W), F32),
            pltpu.VMEM((N_COL, SEND_ROWS, WW), BF16),
            pltpu.VMEM((N_COL, SEND_ROWS, WW), BF16),
            pltpu.VMEM((2 * RR * ITEMS, W), F32),
            pltpu.VMEM((2 * RR * SP, W), F32),
            pltpu.VMEM((SP, ITEMS), BF16),
            pltpu.VMEM((16, WW), F32),
            pltpu.VMEM((2 * PER * CS, W), F32),
            pltpu.VMEM((CHUNKS * Y_ROWS, W), BF16),
            pltpu.VMEM((CHUNKS * Y_ROWS, W), BF16),
            dma((FB // GROUP,)),
            dma((2,)),
            dma((2,)),
            dma((CHUNKS, N_COL)),
            dma((CHUNKS, N_COL)),
            dma((CHUNKS,)),
            dma((CHUNKS,)),
            pltpu.SemaphoreType.REGULAR,
        ],
        compiler_params=pltpu.CompilerParams(
            collective_id=0, has_side_effects=True, vmem_limit_bytes=52 * 2**20
        ),
        name="galerkin",
    )(
        a_cols,
        outbound_term_lists,
        send_count,
        contrib_slot,
        keep,
        contrib_slot,
        contrib_peer,
        p_blocks,
        a_blocks,
    )


def solution(mesh):
    placed = (
        P("row", "col", None, None),
        P("row", "col", None),
        P("row", None, "col"),
        P("row", "col"),
        P("row", "col"),
        P("row", "col", None),
        P("row", "col"),
        P(),
    )
    return jax.shard_map(
        on_device, mesh=mesh, in_specs=placed, out_specs=P("row", None, "col"), check_vma=False
    )
```

```python
import jax
import jax.numpy as jnp
from jax import lax
from jax.experimental import pallas as pl
from jax.experimental.pallas import tpu as pltpu
from jax.sharding import PartitionSpec as P

B = 64
KA = 27
FB = 32
H = 8
ITEMS = 864
CAP = 13
CS = 54
N_ROW = 8
N_COL = 16
SIDE = 4
KP = 14
W = 2 * B
WW = 4 * B
RR = B // 4
SP = 64
NONE = 63
GROUP = 4
KS = 32
TERMS = FB * KS
Q_BEFORE = 4
CHUNK_TILES = (0, 5, 8, 11, 14)
CHUNKS = 4
SEND_ROWS = 14 * 16
PER = RR // CHUNKS
Y_ROWS = 2 * PER * CS

F32 = jnp.float32
BF16 = jnp.bfloat16
MESH = pl.DeviceIdType.MESH


def iota(shape, dim):
    return lax.broadcasted_iota(jnp.int32, shape, dim)


def packed(pair):
    return jnp.where(iota((2 * RR, W), 1) < B, pair[: 2 * RR], pair[2 * RR :])


def side_by_side(upper, lower):
    return jnp.concatenate([upper, lower], axis=1)


def fill_table(table_ref, at, tiles, load):
    for m in range(tiles):
        tile = load(m).astype(F32)
        turned = pltpu.roll(tile, B, 1)
        low = iota(tile.shape, 1) < B
        table_ref[at + 2 * m] = jnp.where(low, tile, turned).astype(BF16)
        table_ref[at + 2 * m + 1] = jnp.where(low, turned, tile).astype(BF16)


def kernel(
    cols_ref,
    items_ref,
    counts_ref,
    slot_ref,
    keep_ref,
    peer_ref,
    p_any,
    a_ref,
    out_any,
    out_ref,
    cols,
    items,
    counts,
    slot_scalars,
    keep,
    slot_row,
    peer_row,
    p_ref,
    a_buf,
    q_buf,
    table,
    halo_left,
    halo_right,
    stage,
    outgoing,
    arrived,
    mixed,
    terms,
    acc,
    own_hot,
    slot_rows,
    y_stage,
    y_out,
    y_in,
    a_sems,
    halo_send,
    halo_recv,
    sends,
    recvs,
    y_send,
    y_recv,
    ready,
    in_sems,
    out_sems,
):
    row = lax.axis_index("row")
    col = lax.axis_index("col")
    z = col // SIDE
    x = col % SIDE
    partner = ((row + N_ROW // 2) % N_ROW, col)
    before = (row, (col + N_COL - 1) % N_COL)
    after = (row, (col + 1) % N_COL)

    def a_copy(g):
        part = pl.ds(g * GROUP, GROUP)
        return pltpu.make_async_copy(a_ref.at[0, part], a_buf.at[part], a_sems.at[g])

    barrier = pltpu.get_barrier_semaphore()

    def greet(peer):
        pl.semaphore_signal(barrier, inc=1, device_id=(row, peer), device_id_type=MESH)

    at_edge = jnp.logical_or(x == 0, x == SIDE - 1)

    @pl.when(x == 0)
    def _():
        greet((col + N_COL - 1) % N_COL)

    @pl.when(x == SIDE - 1)
    def _():
        greet((col + 1) % N_COL)

    for d in range(1, SIDE):
        greet(z * SIDE + (x + d) % SIDE)
    for d in range(1, SIDE):
        greet(((z + d) % SIDE) * SIDE + x)
    pl.semaphore_signal(barrier, inc=1, device_id=partner, device_id_type=MESH)

    fetched = [
        pltpu.make_async_copy(source, here, in_sems.at[n])
        for n, (source, here) in enumerate(
            (
                (p_any, p_ref),
                (slot_ref, slot_row),
                (peer_ref, peer_row),
                (cols_ref, cols),
                (items_ref, items),
                (counts_ref, counts),
                (slot_ref, slot_scalars),
                (keep_ref, keep),
            )
        )
    ]
    for copy in fetched:
        copy.start()

    @pl.loop(0, FB // GROUP)
    def _(g):
        a_copy(g).start()

    for copy in fetched:
        copy.wait()

    fill_table(table, H, FB // 2, lambda m: p_ref[0, :, m * W : (m + 1) * W])
    own_slots = jnp.concatenate(
        [
            jnp.where(peer_row[...] == col, slot_row[...], NONE),
            jnp.full((1, TERMS - ITEMS), NONE, jnp.int32),
        ],
        axis=1,
    )
    place = iota((1, TERMS), 1)
    spread = jnp.full((1, TERMS), NONE, jnp.int32)
    for i in range(FB):
        inside = jnp.logical_and(place >= i * KS, place < i * KS + KA)
        moved = pltpu.roll(own_slots, i * (KS - KA), 1) if i else own_slots
        spread = jnp.where(inside, moved, spread)
    own_hot[...] = jnp.where(spread == iota((SP, TERMS), 0), 1.0, 0.0).astype(BF16)
    mixed[...] = jnp.zeros_like(mixed)
    arrived[col] = jnp.zeros((SEND_ROWS, WW), BF16)

    def form_q(g):
        a_copy(g).wait()
        for m in range(GROUP // 2):
            pair = p_ref[0, :, pl.ds(pl.multiple_of((g * (GROUP // 2) + m) * W, W), W)]
            for h in range(2):
                i = g * GROUP + 2 * m + h
                q = lax.dot_general(
                    pair[:, h * B : (h + 1) * B],
                    a_buf[i],
                    (((0,), (0,)), ((), ())),
                    preferred_element_type=F32,
                )
                q = q.astype(BF16)
                for kp in range(KP - 1):
                    q_buf[i * KP + kp] = q[:, kp * W : (kp + 1) * W]
                q_buf[i * KP + KP - 1, :, :B] = q[:, (KP - 1) * W :]
                q_buf[i * KP + KP - 1, :, B:] = jnp.zeros((B, B), BF16)

    pl.loop(0, Q_BEFORE)(form_q)
    pl.semaphore_wait(barrier, 2 * SIDE - 1 + jnp.where(at_edge, 1, 0))
    for d in range(1, SIDE):
        pl.semaphore_signal(
            ready,
            inc=1,
            device_id=(row, ((z + d) % SIDE) * SIDE + x),
            device_id_type=MESH,
        )
    to_after = pltpu.make_async_remote_copy(
        src_ref=p_ref.at[0, :, pl.ds((FB - H) * B, H * B)],
        dst_ref=halo_left,
        send_sem=halo_send.at[0],
        recv_sem=halo_recv.at[0],
        device_id=after,
        device_id_type=MESH,
    )
    to_before = pltpu.make_async_remote_copy(
        src_ref=p_ref.at[0, :, pl.ds(0, H * B)],
        dst_ref=halo_right,
        send_sem=halo_send.at[1],
        recv_sem=halo_recv.at[1],
        device_id=before,
        device_id_type=MESH,
    )
    to_after.start()
    to_before.start()
    pl.loop(Q_BEFORE, FB // GROUP)(form_q)
    to_after.wait()
    to_before.wait()
    pl.semaphore_wait(ready, SIDE - 1)
    has_left = jnp.where(col > 0, 1.0, 0.0).astype(F32)
    has_right = jnp.where(col < N_COL - 1, 1.0, 0.0).astype(F32)
    fill_table(
        table, 0, H // 2, lambda m: halo_left[:, m * W : (m + 1) * W].astype(F32) * has_left
    )
    fill_table(
        table, H + FB, H // 2, lambda m: halo_right[:, m * W : (m + 1) * W].astype(F32) * has_right
    )

    zero = jnp.zeros((B, W), BF16)

    def peer_of(n):
        dz = (2 + n // SIDE) % SIDE
        dx = (2 + n % SIDE) % SIDE
        return ((z + dz) % SIDE) * SIDE + (x + dx) % SIDE

    def source_of(n):
        dz = (2 + n // SIDE) % SIDE
        dx = (2 + n % SIDE) % SIDE
        return ((z + SIDE - dz) % SIDE) * SIDE + (x + SIDE - dx) % SIDE

    def send_copy(chunk, n):
        first, last = CHUNK_TILES[chunk], CHUNK_TILES[chunk + 1]
        part = pl.ds(first * 16, (last - first) * 16)
        peer = peer_of(n)
        return pltpu.make_async_remote_copy(
            src_ref=outgoing.at[peer, part],
            dst_ref=arrived.at[col, part],
            send_sem=sends.at[chunk, n],
            recv_sem=recvs.at[chunk, n],
            device_id=(row, peer),
            device_id_type=MESH,
        )

    def recv_copy(chunk, n):
        first, last = CHUNK_TILES[chunk], CHUNK_TILES[chunk + 1]
        part = pl.ds(first * 16, (last - first) * 16)
        peer = source_of(n)
        return pltpu.make_async_remote_copy(
            src_ref=outgoing.at[peer, part],
            dst_ref=arrived.at[peer, part],
            send_sem=sends.at[chunk, n],
            recv_sem=recvs.at[chunk, n],
            device_id=(row, peer),
            device_id_type=MESH,
        )

    place = (iota((16, WW), 0) * 16 + iota((16, WW), 1) % 16) % CAP

    def list_terms(n):
        p = peer_of(n)
        tags = jnp.full((16, WW), NONE, jnp.int32)
        for j in range(CAP):
            e = items[j, 0, p]
            i = e // KA
            k = e - i * KA
            kp = k // 2
            odd = (k - 2 * kp) == 1
            tile = q_buf[i * KP + kp]
            t = table[cols[k, 0, i]]
            rhs = jnp.concatenate([jnp.where(odd, zero, t), jnp.where(odd, t, zero)], axis=0)
            g = jnp.dot(tile, rhs, preferred_element_type=F32)
            stage[pl.ds(j, 2 * RR, stride=CAP), :] = packed(g)
            slot = jnp.where(j < counts[0, p], slot_scalars[0, e], NONE)
            tags = jnp.where(place == j, slot, tags)
        outgoing[p, pl.ds(0, 16)] = tags.astype(F32).astype(BF16)
        outgoing[p, pl.ds(16, RR * CAP)] = side_by_side(
            stage[: RR * CAP, :], stage[RR * CAP :, :]
        ).astype(BF16)
        send_copy(0, n).start()

    pl.loop(0, 10)(list_terms)
    pl.loop(11, N_COL)(list_terms)
    for chunk in range(1, CHUNKS):
        for span in ((0, 10), (11, N_COL)):

            @pl.loop(*span)
            def _(n):
                send_copy(chunk, n).start()

    def own_terms(i, buf):
        for kp in range(KP):
            tile = q_buf[i * KP + kp]
            t0 = table[cols[2 * kp, 0, i]]
            if 2 * kp + 1 < KA:
                t1 = table[cols[2 * kp + 1, 0, i]]
                rhs = jnp.concatenate(
                    [jnp.concatenate([t0, zero], axis=1), jnp.concatenate([zero, t1], axis=1)],
                    axis=0,
                )
            else:
                rhs = jnp.concatenate([t0, zero], axis=0)
            g = jnp.dot(tile, rhs, preferred_element_type=F32)
            mixed[pl.ds(buf + 2 * kp, 2 * RR, stride=KS), :] = packed(g[:, :W])
            if 2 * kp + 1 < KA:
                mixed[pl.ds(buf + 2 * kp + 1, 2 * RR, stride=KS), :] = packed(g[:, W:])
        rows = pl.ds(pl.multiple_of(i * KS, KS), KS)
        for r in range(2 * RR):
            terms[r, rows, :] = mixed[buf + r * KS : buf + (r + 1) * KS, :].astype(BF16)

    @pl.loop(0, FB // 2)
    def _(m):
        own_terms(2 * m, 0)
        own_terms(2 * m + 1, 2 * RR * KS)

    def own_sum(chunk):
        for r in range(chunk * PER, (chunk + 1) * PER):
            total = jnp.dot(
                own_hot[...], side_by_side(terms[r], terms[RR + r]), preferred_element_type=F32
            )
            acc[r * SP : (r + 1) * SP, :] += total[:, :W]
            acc[(RR + r) * SP : (RR + r + 1) * SP, :] += total[:, W:]

    acc[...] = jnp.zeros_like(acc)

    lane = iota((1, WW), 1)

    def y_copy(chunk):
        part = pl.ds(chunk * Y_ROWS, Y_ROWS)
        return pltpu.make_async_remote_copy(
            src_ref=y_out.at[part],
            dst_ref=y_in.at[part],
            send_sem=y_send.at[chunk],
            recv_sem=y_recv.at[chunk],
            device_id=partner,
            device_id_type=MESH,
        )

    def merge(chunk):
        for span in ((0, 10), (11, N_COL)):

            @pl.loop(*span)
            def _(n):
                recv_copy(chunk, n).wait_recv()

        if chunk == 0:
            group = iota((16, WW), 1) // 16
            rows = jnp.full((16, WW), float(NONE), F32)
            for src in range(N_COL):
                tags = arrived[src, 0:16, :].astype(F32)
                mine = jnp.logical_and(group == src, src != col)
                rows = jnp.where(mine, tags, rows)
            slot_rows[...] = rows
        for tile in range(CHUNK_TILES[chunk], CHUNK_TILES[chunk + 1]):
            if tile == 0:
                continue
            tau = tile - 1
            first = tau * 16 // CAP
            last = (tau * 16 + 15) // CAP
            slots = slot_rows[tau % CAP : tau % CAP + 1, :]
            r_of = (tau * 16 + lane % 16) // CAP
            values = arrived[:, tile * 16 : tile * 16 + 16, :].reshape(WW, WW)
            sub = iota((SP, WW), 0).astype(F32)
            hot = [
                jnp.where(jnp.where(r_of == r, slots, -1.0) == sub, 1.0, 0.0).astype(BF16)
                for r in range(first, last + 1)
            ]
            more = jnp.dot(jnp.concatenate(hot, axis=0), values, preferred_element_type=F32)
            acc[first * SP : (last + 1) * SP, :] += more[:, :W]
            acc[(RR + first) * SP : (RR + last + 1) * SP, :] += more[:, W:]
        for h in range(2):
            for n in range(PER):
                at = (h * RR + chunk * PER + n) * SP
                y_stage[(h * PER + n) * CS : (h * PER + n + 1) * CS, :] = acc[at : at + CS, :]
        y_out[chunk * Y_ROWS : (chunk + 1) * Y_ROWS, :] = y_stage[...].astype(BF16)
        y_copy(chunk).start()

    weight = keep[row].astype(F32)

    def finish(chunk):
        y_copy(chunk).wait_recv()
        y_stage[...] = y_in[chunk * Y_ROWS : (chunk + 1) * Y_ROWS, :].astype(F32)
        for h in range(2):
            for n in range(PER):
                at = (h * RR + chunk * PER + n) * SP
                more = y_stage[(h * PER + n) * CS : (h * PER + n + 1) * CS, :]
                acc[at : at + CS, :] = (acc[at : at + CS, :] + more) * weight
        low = iota((PER, W), 1) < B
        at = chunk * PER
        for m in range(CS // 2):
            lanes = slice(m * W, (m + 1) * W)
            for half in range(2):
                up = half * RR + at
                a = acc[pl.ds(up * SP + 2 * m, PER, stride=SP), :]
                b = acc[pl.ds(up * SP + 2 * m + 1, PER, stride=SP), :]
                out_ref[0, up : up + PER, lanes] = jnp.where(low, a, pltpu.roll(b, B, 1))
                up = 2 * RR + up
                out_ref[0, up : up + PER, lanes] = jnp.where(low, pltpu.roll(a, B, 1), b)

    def out_copy(n):
        part = pl.ds(n * 8, 8)
        return pltpu.make_async_copy(
            out_ref.at[0, part], out_any.at[0, part], out_sems.at[n]
        )

    for chunk in range(CHUNKS):
        own_sum(chunk)
        merge(chunk)
    for chunk in range(CHUNKS):
        finish(chunk)
        if chunk == 1:
            for n in range(0, 8, 2):
                out_copy(n).start()
    for n in range(1, 8, 2):
        out_copy(n).start()
    for n in range(8):
        out_copy(n).wait()
    for chunk in range(CHUNKS):
        y_copy(chunk).wait_send()
        for span in ((0, 10), (11, N_COL)):

            @pl.loop(*span)
            def _(n):
                send_copy(chunk, n).wait_send()


def on_device(
    a_blocks, a_cols, p_blocks, contrib_peer, contrib_slot, outbound_term_lists, send_count, keep
):
    dma = pltpu.SemaphoreType.DMA
    return pl.pallas_call(
        kernel,
        in_specs=[pl.BlockSpec(memory_space=pl.ANY)] * 8,
        out_specs=pl.BlockSpec(memory_space=pl.ANY),
        out_shape=jax.ShapeDtypeStruct((1, B, CS * B), F32),
        scratch_shapes=[
            pltpu.VMEM((1, B, CS * B), F32),
            pltpu.SMEM((KA, 1, FB), jnp.int32),
            pltpu.SMEM((CAP, 1, N_COL), jnp.int32),
            pltpu.SMEM(send_count.shape, jnp.int32),
            pltpu.SMEM(contrib_slot.shape, jnp.int32),
            pltpu.SMEM(keep.shape, jnp.int32),
            pltpu.VMEM(contrib_slot.shape, jnp.int32),
            pltpu.VMEM(contrib_peer.shape, jnp.int32),
            pltpu.VMEM(p_blocks.shape, BF16),
            pltpu.VMEM((FB, B, KA * B), BF16),
            pltpu.VMEM((FB * KP, B, W), BF16),
            pltpu.VMEM((FB + 2 * H, B, W), BF16),
            pltpu.VMEM((B, H * B), BF16),
            pltpu.VMEM((B, H * B), BF16),
            pltpu.VMEM((2 * RR * CAP, W), F32),
            pltpu.VMEM((N_COL, SEND_ROWS, WW), BF16),
            pltpu.VMEM((N_COL, SEND_ROWS, WW), BF16),
            pltpu.VMEM((4 * RR * KS, W), F32),
            pltpu.VMEM((2 * RR, TERMS, W), BF16),
            pltpu.VMEM((2 * RR * SP, W), F32),
            pltpu.VMEM((SP, TERMS), BF16),
            pltpu.VMEM((16, WW), F32),
            pltpu.VMEM((2 * PER * CS, W), F32),
            pltpu.VMEM((CHUNKS * Y_ROWS, W), BF16),
            pltpu.VMEM((CHUNKS * Y_ROWS, W), BF16),
            dma((FB // GROUP,)),
            dma((2,)),
            dma((2,)),
            dma((CHUNKS, N_COL)),
            dma((CHUNKS, N_COL)),
            dma((CHUNKS,)),
            dma((CHUNKS,)),
            pltpu.SemaphoreType.REGULAR,
            dma((8,)),
            dma((8,)),
        ],
        compiler_params=pltpu.CompilerParams(
            collective_id=0, has_side_effects=True, vmem_limit_bytes=62 * 2**20
        ),
        name="galerkin",
    )(
        jnp.transpose(a_cols, (2, 0, 1)),
        jnp.transpose(outbound_term_lists, (2, 0, 1)),
        send_count,
        contrib_slot,
        keep,
        contrib_peer,
        p_blocks,
        a_blocks,
    )


def solution(mesh):
    placed = (
        P("row", "col", None, None),
        P("row", "col", None),
        P("row", None, "col"),
        P("row", "col"),
        P("row", "col"),
        P("row", "col", None),
        P("row", "col"),
        P(),
    )
    return jax.shard_map(
        on_device, mesh=mesh, in_specs=placed, out_specs=P("row", None, "col"), check_vma=False
    )
```

```python
import jax
import jax.numpy as jnp
from jax import lax
from jax.experimental import pallas as pl
from jax.experimental.pallas import tpu as pltpu
from jax.sharding import PartitionSpec as P

B = 64
KA = 27
FB = 32
H = 8
ITEMS = 864
CAP = 13
CS = 54
N_ROW = 8
N_COL = 16
SIDE = 4
KP = 14
W = 2 * B
WW = 4 * B
RR = B // 4
SP = 64
NONE = 63
GROUP = 4
KS = 32
MS = 40
TERMS = FB * KS
Q_BEFORE = 4
CHUNK_TILES = (0, 5, 8, 11, 14)
CHUNKS = 4
SEND_ROWS = 14 * 16
PER = RR // CHUNKS
Y_ROWS = 2 * PER * CS

F32 = jnp.float32
BF16 = jnp.bfloat16
MESH = pl.DeviceIdType.MESH


def iota(shape, dim):
    return lax.broadcasted_iota(jnp.int32, shape, dim)


def packed(pair):
    return jnp.where(iota((2 * RR, W), 1) < B, pair[: 2 * RR], pair[2 * RR :])


def side_by_side(upper, lower):
    return jnp.concatenate([upper, lower], axis=1)


def fill_table(table_ref, at, tiles, load):
    for m in range(tiles):
        tile = load(m).astype(F32)
        turned = pltpu.roll(tile, B, 1)
        low = iota(tile.shape, 1) < B
        table_ref[at + 2 * m] = jnp.where(low, tile, turned).astype(BF16)
        table_ref[at + 2 * m + 1] = jnp.where(low, turned, tile).astype(BF16)


def kernel(
    cols_ref,
    items_ref,
    counts_ref,
    slot_ref,
    keep_ref,
    peer_ref,
    p_any,
    a_ref,
    out_any,
    out_ref,
    cols,
    items,
    counts,
    slot_scalars,
    keep,
    slot_row,
    peer_row,
    p_ref,
    a_buf,
    q_buf,
    table,
    halo_left,
    halo_right,
    stage,
    outgoing,
    arrived,
    mixed,
    mixed_next,
    terms,
    acc,
    own_hot,
    slot_rows,
    y_stage,
    y_out,
    y_in,
    a_sems,
    halo_send,
    halo_recv,
    sends,
    recvs,
    y_send,
    y_recv,
    ready,
    in_sems,
    out_sems,
):
    row = lax.axis_index("row")
    col = lax.axis_index("col")
    z = col // SIDE
    x = col % SIDE
    partner = ((row + N_ROW // 2) % N_ROW, col)
    before = (row, (col + N_COL - 1) % N_COL)
    after = (row, (col + 1) % N_COL)

    def a_copy(g):
        part = pl.ds(g * GROUP, GROUP)
        return pltpu.make_async_copy(a_ref.at[0, part], a_buf.at[part], a_sems.at[g])

    barrier = pltpu.get_barrier_semaphore()

    def greet(peer):
        pl.semaphore_signal(barrier, inc=1, device_id=(row, peer), device_id_type=MESH)

    at_edge = jnp.logical_or(x == 0, x == SIDE - 1)

    @pl.when(x == 0)
    def _():
        greet((col + N_COL - 1) % N_COL)

    @pl.when(x == SIDE - 1)
    def _():
        greet((col + 1) % N_COL)

    for d in range(1, SIDE):
        greet(z * SIDE + (x + d) % SIDE)
    for d in range(1, SIDE):
        greet(((z + d) % SIDE) * SIDE + x)
    pl.semaphore_signal(barrier, inc=1, device_id=partner, device_id_type=MESH)

    fetched = [
        pltpu.make_async_copy(source, here, in_sems.at[n])
        for n, (source, here) in enumerate(
            (
                (p_any, p_ref),
                (slot_ref, slot_row),
                (peer_ref, peer_row),
                (cols_ref, cols),
                (items_ref, items),
                (counts_ref, counts),
                (slot_ref, slot_scalars),
                (keep_ref, keep),
            )
        )
    ]
    for copy in fetched:
        copy.start()

    @pl.loop(0, FB // GROUP)
    def _(g):
        a_copy(g).start()

    for copy in fetched:
        copy.wait()

    fill_table(table, H, FB // 2, lambda m: p_ref[0, :, m * W : (m + 1) * W])
    own_slots = jnp.concatenate(
        [
            jnp.where(peer_row[...] == col, slot_row[...], NONE),
            jnp.full((1, TERMS - ITEMS), NONE, jnp.int32),
        ],
        axis=1,
    )
    place = iota((1, TERMS), 1)
    spread = jnp.full((1, TERMS), NONE, jnp.int32)
    for i in range(FB):
        inside = jnp.logical_and(place >= i * KS, place < i * KS + KA)
        moved = pltpu.roll(own_slots, i * (KS - KA), 1) if i else own_slots
        spread = jnp.where(inside, moved, spread)
    own_hot[...] = jnp.where(spread == iota((SP, TERMS), 0), 1.0, 0.0).astype(BF16)
    mixed[...] = jnp.zeros_like(mixed)
    mixed_next[...] = jnp.zeros_like(mixed_next)
    arrived[col] = jnp.zeros((SEND_ROWS, WW), BF16)

    def form_q(g):
        a_copy(g).wait()
        for m in range(GROUP // 2):
            pair = p_ref[0, :, pl.ds(pl.multiple_of((g * (GROUP // 2) + m) * W, W), W)]
            for h in range(2):
                i = g * GROUP + 2 * m + h
                q = lax.dot_general(
                    pair[:, h * B : (h + 1) * B],
                    a_buf[i],
                    (((0,), (0,)), ((), ())),
                    preferred_element_type=F32,
                )
                q = q.astype(BF16)
                for kp in range(KP - 1):
                    q_buf[i * KP + kp] = q[:, kp * W : (kp + 1) * W]
                q_buf[i * KP + KP - 1, :, :B] = q[:, (KP - 1) * W :]
                q_buf[i * KP + KP - 1, :, B:] = jnp.zeros((B, B), BF16)

    pl.loop(0, Q_BEFORE)(form_q)
    pl.semaphore_wait(barrier, 2 * SIDE - 1 + jnp.where(at_edge, 1, 0))
    for d in range(1, SIDE):
        pl.semaphore_signal(
            ready,
            inc=1,
            device_id=(row, ((z + d) % SIDE) * SIDE + x),
            device_id_type=MESH,
        )
    to_after = pltpu.make_async_remote_copy(
        src_ref=p_ref.at[0, :, pl.ds((FB - H) * B, H * B)],
        dst_ref=halo_left,
        send_sem=halo_send.at[0],
        recv_sem=halo_recv.at[0],
        device_id=after,
        device_id_type=MESH,
    )
    to_before = pltpu.make_async_remote_copy(
        src_ref=p_ref.at[0, :, pl.ds(0, H * B)],
        dst_ref=halo_right,
        send_sem=halo_send.at[1],
        recv_sem=halo_recv.at[1],
        device_id=before,
        device_id_type=MESH,
    )
    to_after.start()
    to_before.start()
    pl.loop(Q_BEFORE, FB // GROUP)(form_q)
    to_after.wait()
    to_before.wait()
    pl.semaphore_wait(ready, SIDE - 1)
    has_left = jnp.where(col > 0, 1.0, 0.0).astype(F32)
    has_right = jnp.where(col < N_COL - 1, 1.0, 0.0).astype(F32)
    fill_table(
        table, 0, H // 2, lambda m: halo_left[:, m * W : (m + 1) * W].astype(F32) * has_left
    )
    fill_table(
        table, H + FB, H // 2, lambda m: halo_right[:, m * W : (m + 1) * W].astype(F32) * has_right
    )

    zero = jnp.zeros((B, W), BF16)

    def peer_of(n):
        dz = (2 + n // SIDE) % SIDE
        dx = (2 + n % SIDE) % SIDE
        return ((z + dz) % SIDE) * SIDE + (x + dx) % SIDE

    def source_of(n):
        dz = (2 + n // SIDE) % SIDE
        dx = (2 + n % SIDE) % SIDE
        return ((z + SIDE - dz) % SIDE) * SIDE + (x + SIDE - dx) % SIDE

    def send_copy(chunk, n):
        first, last = CHUNK_TILES[chunk], CHUNK_TILES[chunk + 1]
        part = pl.ds(first * 16, (last - first) * 16)
        peer = peer_of(n)
        return pltpu.make_async_remote_copy(
            src_ref=outgoing.at[peer, part],
            dst_ref=arrived.at[col, part],
            send_sem=sends.at[chunk, n],
            recv_sem=recvs.at[chunk, n],
            device_id=(row, peer),
            device_id_type=MESH,
        )

    def recv_copy(chunk, n):
        first, last = CHUNK_TILES[chunk], CHUNK_TILES[chunk + 1]
        part = pl.ds(first * 16, (last - first) * 16)
        peer = source_of(n)
        return pltpu.make_async_remote_copy(
            src_ref=outgoing.at[peer, part],
            dst_ref=arrived.at[peer, part],
            send_sem=sends.at[chunk, n],
            recv_sem=recvs.at[chunk, n],
            device_id=(row, peer),
            device_id_type=MESH,
        )

    place = (iota((16, WW), 0) * 16 + iota((16, WW), 1) % 16) % CAP

    def list_terms(n):
        p = peer_of(n)
        tags = jnp.full((16, WW), NONE, jnp.int32)
        for j in range(CAP):
            e = items[j, 0, p]
            i = e // KA
            k = e - i * KA
            kp = k // 2
            odd = (k - 2 * kp) == 1
            tile = q_buf[i * KP + kp]
            t = table[cols[k, 0, i]]
            rhs = jnp.concatenate([jnp.where(odd, zero, t), jnp.where(odd, t, zero)], axis=0)
            g = jnp.dot(tile, rhs, preferred_element_type=F32)
            stage[pl.ds(j, 2 * RR, stride=CAP), :] = packed(g)
            slot = jnp.where(j < counts[0, p], slot_scalars[0, e], NONE)
            tags = jnp.where(place == j, slot, tags)
        outgoing[p, pl.ds(0, 16)] = tags.astype(F32).astype(BF16)
        outgoing[p, pl.ds(16, RR * CAP)] = side_by_side(
            stage[: RR * CAP, :], stage[RR * CAP :, :]
        ).astype(BF16)
        send_copy(0, n).start()

    pl.loop(0, 10)(list_terms)
    pl.loop(11, N_COL)(list_terms)
    for chunk in range(1, CHUNKS):
        for span in ((0, 10), (11, N_COL)):

            @pl.loop(*span)
            def _(n):
                send_copy(chunk, n).start()

    def own_terms(i, here, there):
        rows = pl.ds(pl.multiple_of(((i + FB - 1) % FB) * KS, KS), KS)
        for kp in range(KP):
            tile = q_buf[i * KP + kp]
            t0 = table[cols[2 * kp, 0, i]]
            if 2 * kp + 1 < KA:
                t1 = table[cols[2 * kp + 1, 0, i]]
                rhs = jnp.concatenate(
                    [jnp.concatenate([t0, zero], axis=1), jnp.concatenate([zero, t1], axis=1)],
                    axis=0,
                )
            else:
                rhs = jnp.concatenate([t0, zero], axis=0)
            g = jnp.dot(tile, rhs, preferred_element_type=F32)
            here[pl.ds(2 * kp, 2 * RR, stride=MS), :] = packed(g[:, :W])
            if 2 * kp + 1 < KA:
                here[pl.ds(2 * kp + 1, 2 * RR, stride=MS), :] = packed(g[:, W:])
            for r in range(2 * RR * kp // KP, 2 * RR * (kp + 1) // KP):
                terms[r, rows, :] = there[r * MS : r * MS + KS, :].astype(BF16)

    @pl.loop(0, FB // 2)
    def _(m):
        own_terms(2 * m, mixed, mixed_next)
        own_terms(2 * m + 1, mixed_next, mixed)

    for r in range(2 * RR):
        terms[r, (FB - 1) * KS : FB * KS, :] = mixed_next[r * MS : r * MS + KS, :].astype(BF16)

    def own_sum(chunk):
        for r in range(chunk * PER, (chunk + 1) * PER):
            total = jnp.dot(
                own_hot[...], side_by_side(terms[r], terms[RR + r]), preferred_element_type=F32
            )
            acc[r * SP : (r + 1) * SP, :] += total[:, :W]
            acc[(RR + r) * SP : (RR + r + 1) * SP, :] += total[:, W:]

    acc[...] = jnp.zeros_like(acc)

    lane = iota((1, WW), 1)

    def y_copy(chunk):
        part = pl.ds(chunk * Y_ROWS, Y_ROWS)
        return pltpu.make_async_remote_copy(
            src_ref=y_out.at[part],
            dst_ref=y_in.at[part],
            send_sem=y_send.at[chunk],
            recv_sem=y_recv.at[chunk],
            device_id=partner,
            device_id_type=MESH,
        )

    def merge(chunk):
        for span in ((0, 10), (11, N_COL)):

            @pl.loop(*span)
            def _(n):
                recv_copy(chunk, n).wait_recv()

        if chunk == 0:
            group = iota((16, WW), 1) // 16
            rows = jnp.full((16, WW), float(NONE), F32)
            for src in range(N_COL):
                tags = arrived[src, 0:16, :].astype(F32)
                mine = jnp.logical_and(group == src, src != col)
                rows = jnp.where(mine, tags, rows)
            slot_rows[...] = rows
        for tile in range(CHUNK_TILES[chunk], CHUNK_TILES[chunk + 1]):
            if tile == 0:
                continue
            tau = tile - 1
            first = tau * 16 // CAP
            last = (tau * 16 + 15) // CAP
            slots = slot_rows[tau % CAP : tau % CAP + 1, :]
            r_of = (tau * 16 + lane % 16) // CAP
            values = arrived[:, tile * 16 : tile * 16 + 16, :].reshape(WW, WW)
            sub = iota((SP, WW), 0).astype(F32)
            hot = [
                jnp.where(jnp.where(r_of == r, slots, -1.0) == sub, 1.0, 0.0).astype(BF16)
                for r in range(first, last + 1)
            ]
            more = jnp.dot(jnp.concatenate(hot, axis=0), values, preferred_element_type=F32)
            acc[first * SP : (last + 1) * SP, :] += more[:, :W]
            acc[(RR + first) * SP : (RR + last + 1) * SP, :] += more[:, W:]
        for h in range(2):
            for n in range(PER):
                at = (h * RR + chunk * PER + n) * SP
                y_stage[(h * PER + n) * CS : (h * PER + n + 1) * CS, :] = acc[at : at + CS, :]
        y_out[chunk * Y_ROWS : (chunk + 1) * Y_ROWS, :] = y_stage[...].astype(BF16)
        y_copy(chunk).start()

    weight = keep[row].astype(F32)

    def finish(chunk):
        y_copy(chunk).wait_recv()
        y_stage[...] = y_in[chunk * Y_ROWS : (chunk + 1) * Y_ROWS, :].astype(F32)
        for h in range(2):
            for n in range(PER):
                at = (h * RR + chunk * PER + n) * SP
                more = y_stage[(h * PER + n) * CS : (h * PER + n + 1) * CS, :]
                acc[at : at + CS, :] = (acc[at : at + CS, :] + more) * weight
        low = iota((PER, W), 1) < B
        at = chunk * PER
        for m in range(CS // 2):
            lanes = slice(m * W, (m + 1) * W)
            for half in range(2):
                up = half * RR + at
                a = acc[pl.ds(up * SP + 2 * m, PER, stride=SP), :]
                b = acc[pl.ds(up * SP + 2 * m + 1, PER, stride=SP), :]
                out_ref[0, up : up + PER, lanes] = jnp.where(low, a, pltpu.roll(b, B, 1))
                up = 2 * RR + up
                out_ref[0, up : up + PER, lanes] = jnp.where(low, pltpu.roll(a, B, 1), b)

    def out_copy(n):
        part = pl.ds(n * 8, 8)
        return pltpu.make_async_copy(
            out_ref.at[0, part], out_any.at[0, part], out_sems.at[n]
        )

    for chunk in range(CHUNKS):
        own_sum(chunk)
        merge(chunk)
    for chunk in range(CHUNKS):
        finish(chunk)
        if chunk == 1:
            for n in range(0, 8, 2):
                out_copy(n).start()
    for n in range(1, 8, 2):
        out_copy(n).start()
    for n in range(8):
        out_copy(n).wait()
    for chunk in range(CHUNKS):
        y_copy(chunk).wait_send()
        for span in ((0, 10), (11, N_COL)):

            @pl.loop(*span)
            def _(n):
                send_copy(chunk, n).wait_send()


def on_device(
    a_blocks, a_cols, p_blocks, contrib_peer, contrib_slot, outbound_term_lists, send_count, keep
):
    dma = pltpu.SemaphoreType.DMA
    return pl.pallas_call(
        kernel,
        in_specs=[pl.BlockSpec(memory_space=pl.ANY)] * 8,
        out_specs=pl.BlockSpec(memory_space=pl.ANY),
        out_shape=jax.ShapeDtypeStruct((1, B, CS * B), F32),
        scratch_shapes=[
            pltpu.VMEM((1, B, CS * B), F32),
            pltpu.SMEM((KA, 1, FB), jnp.int32),
            pltpu.SMEM((CAP, 1, N_COL), jnp.int32),
            pltpu.SMEM(send_count.shape, jnp.int32),
            pltpu.SMEM(contrib_slot.shape, jnp.int32),
            pltpu.SMEM(keep.shape, jnp.int32),
            pltpu.VMEM(contrib_slot.shape, jnp.int32),
            pltpu.VMEM(contrib_peer.shape, jnp.int32),
            pltpu.VMEM(p_blocks.shape, BF16),
            pltpu.VMEM((FB, B, KA * B), BF16),
            pltpu.VMEM((FB * KP, B, W), BF16),
            pltpu.VMEM((FB + 2 * H, B, W), BF16),
            pltpu.VMEM((B, H * B), BF16),
            pltpu.VMEM((B, H * B), BF16),
            pltpu.VMEM((2 * RR * CAP, W), F32),
            pltpu.VMEM((N_COL, SEND_ROWS, WW), BF16),
            pltpu.VMEM((N_COL, SEND_ROWS, WW), BF16),
            pltpu.VMEM((2 * RR * MS, W), F32),
            pltpu.VMEM((2 * RR * MS, W), F32),
            pltpu.VMEM((2 * RR, TERMS, W), BF16),
            pltpu.VMEM((2 * RR * SP, W), F32),
            pltpu.VMEM((SP, TERMS), BF16),
            pltpu.VMEM((16, WW), F32),
            pltpu.VMEM((2 * PER * CS, W), F32),
            pltpu.VMEM((CHUNKS * Y_ROWS, W), BF16),
            pltpu.VMEM((CHUNKS * Y_ROWS, W), BF16),
            dma((FB // GROUP,)),
            dma((2,)),
            dma((2,)),
            dma((CHUNKS, N_COL)),
            dma((CHUNKS, N_COL)),
            dma((CHUNKS,)),
            dma((CHUNKS,)),
            pltpu.SemaphoreType.REGULAR,
            dma((8,)),
            dma((8,)),
        ],
        compiler_params=pltpu.CompilerParams(
            collective_id=0, has_side_effects=True, vmem_limit_bytes=62 * 2**20
        ),
        name="galerkin",
    )(
        jnp.transpose(a_cols, (2, 0, 1)),
        jnp.transpose(outbound_term_lists, (2, 0, 1)),
        send_count,
        contrib_slot,
        keep,
        contrib_peer,
        p_blocks,
        a_blocks,
    )


def solution(mesh):
    placed = (
        P("row", "col", None, None),
        P("row", "col", None),
        P("row", None, "col"),
        P("row", "col"),
        P("row", "col"),
        P("row", "col", None),
        P("row", "col"),
        P(),
    )
    return jax.shard_map(
        on_device, mesh=mesh, in_specs=placed, out_specs=P("row", None, "col"), check_vma=False
    )
```

```python
import jax
import jax.numpy as jnp
from jax import lax
from jax.experimental import pallas as pl
from jax.experimental.pallas import tpu as pltpu
from jax.sharding import PartitionSpec as P

B = 64
KA = 27
FB = 32
H = 8
ITEMS = 864
CAP = 13
CS = 54
N_ROW = 8
N_COL = 16
SIDE = 4
KP = 14
W = 2 * B
WW = 4 * B
RR = B // 4
SP = 64
NONE = 63
GROUP = 4
KS = 32
MS = 40
TERMS = FB * KS
Q_BEFORE = 4
CHUNK_TILES = (0, 5, 8, 11, 14)
CHUNKS = 4
SEND_ROWS = 14 * 16
PER = RR // CHUNKS
Y_ROWS = 2 * PER * CS

F32 = jnp.float32
BF16 = jnp.bfloat16
MESH = pl.DeviceIdType.MESH


def iota(shape, dim):
    return lax.broadcasted_iota(jnp.int32, shape, dim)


def packed(pair):
    return jnp.where(iota((2 * RR, W), 1) < B, pair[: 2 * RR], pair[2 * RR :])


def side_by_side(upper, lower):
    return jnp.concatenate([upper, lower], axis=1)


def fill_table(table_ref, at, tiles, load):
    for m in range(tiles):
        tile = load(m).astype(F32)
        turned = pltpu.roll(tile, B, 1)
        low = iota(tile.shape, 1) < B
        table_ref[at + 2 * m] = jnp.where(low, tile, turned).astype(BF16)
        table_ref[at + 2 * m + 1] = jnp.where(low, turned, tile).astype(BF16)


def kernel(
    cols_ref,
    items_ref,
    counts_ref,
    slot_ref,
    keep_ref,
    peer_ref,
    p_any,
    a_ref,
    out_any,
    out_ref,
    cols,
    items,
    counts,
    slot_scalars,
    keep,
    slot_row,
    peer_row,
    p_ref,
    a_buf,
    q_buf,
    table,
    halo_left,
    halo_right,
    stage,
    outgoing,
    arrived,
    mixed,
    mixed_next,
    terms,
    acc,
    own_hot,
    slot_rows,
    y_stage,
    y_out,
    y_in,
    a_sems,
    halo_send,
    halo_recv,
    sends,
    recvs,
    y_send,
    y_recv,
    ready,
    in_sems,
    out_sems,
):
    row = lax.axis_index("row")
    col = lax.axis_index("col")
    z = col // SIDE
    x = col % SIDE
    partner = ((row + N_ROW // 2) % N_ROW, col)
    before = (row, (col + N_COL - 1) % N_COL)
    after = (row, (col + 1) % N_COL)

    def a_copy(g):
        part = pl.ds(g * GROUP, GROUP)
        return pltpu.make_async_copy(a_ref.at[0, part], a_buf.at[part], a_sems.at[g])

    barrier = pltpu.get_barrier_semaphore()

    def greet(peer):
        pl.semaphore_signal(barrier, inc=1, device_id=(row, peer), device_id_type=MESH)

    at_edge = jnp.logical_or(x == 0, x == SIDE - 1)

    @pl.when(x == 0)
    def _():
        greet((col + N_COL - 1) % N_COL)

    @pl.when(x == SIDE - 1)
    def _():
        greet((col + 1) % N_COL)

    for d in range(1, SIDE):
        greet(z * SIDE + (x + d) % SIDE)
    for d in range(1, SIDE):
        greet(((z + d) % SIDE) * SIDE + x)
    pl.semaphore_signal(barrier, inc=1, device_id=partner, device_id_type=MESH)

    fetched = [
        pltpu.make_async_copy(source, here, in_sems.at[n])
        for n, (source, here) in enumerate(
            (
                (p_any, p_ref),
                (slot_ref, slot_row),
                (peer_ref, peer_row),
                (cols_ref, cols),
                (items_ref, items),
                (counts_ref, counts),
                (slot_ref, slot_scalars),
                (keep_ref, keep),
            )
        )
    ]
    for copy in fetched:
        copy.start()

    @pl.loop(0, FB // GROUP)
    def _(g):
        a_copy(g).start()

    for copy in fetched:
        copy.wait()

    fill_table(table, H, FB // 2, lambda m: p_ref[0, :, m * W : (m + 1) * W])
    own_slots = jnp.concatenate(
        [
            jnp.where(peer_row[...] == col, slot_row[...], NONE),
            jnp.full((1, TERMS - ITEMS), NONE, jnp.int32),
        ],
        axis=1,
    )
    place = iota((1, TERMS), 1)
    spread = jnp.full((1, TERMS), NONE, jnp.int32)
    for i in range(FB):
        inside = jnp.logical_and(place >= i * KS, place < i * KS + KA)
        moved = pltpu.roll(own_slots, i * (KS - KA), 1) if i else own_slots
        spread = jnp.where(inside, moved, spread)
    own_hot[...] = jnp.where(spread == iota((SP, TERMS), 0), 1.0, 0.0).astype(BF16)
    mixed[...] = jnp.zeros_like(mixed)
    mixed_next[...] = jnp.zeros_like(mixed_next)
    arrived[col] = jnp.zeros((SEND_ROWS, WW), BF16)

    def form_q(g):
        a_copy(g).wait()
        for m in range(GROUP // 2):
            pair = p_ref[0, :, pl.ds(pl.multiple_of((g * (GROUP // 2) + m) * W, W), W)]
            for h in range(2):
                i = g * GROUP + 2 * m + h
                q = lax.dot_general(
                    pair[:, h * B : (h + 1) * B],
                    a_buf[i],
                    (((0,), (0,)), ((), ())),
                    preferred_element_type=F32,
                )
                q = q.astype(BF16)
                for kp in range(KP - 1):
                    q_buf[i * KP + kp] = q[:, kp * W : (kp + 1) * W]
                q_buf[i * KP + KP - 1, :, :B] = q[:, (KP - 1) * W :]
                q_buf[i * KP + KP - 1, :, B:] = jnp.zeros((B, B), BF16)

    pl.loop(0, Q_BEFORE)(form_q)
    pl.semaphore_wait(barrier, 2 * SIDE - 1 + jnp.where(at_edge, 1, 0))
    for d in range(1, SIDE):
        pl.semaphore_signal(
            ready,
            inc=1,
            device_id=(row, ((z + d) % SIDE) * SIDE + x),
            device_id_type=MESH,
        )
    to_after = pltpu.make_async_remote_copy(
        src_ref=p_ref.at[0, :, pl.ds((FB - H) * B, H * B)],
        dst_ref=halo_left,
        send_sem=halo_send.at[0],
        recv_sem=halo_recv.at[0],
        device_id=after,
        device_id_type=MESH,
    )
    to_before = pltpu.make_async_remote_copy(
        src_ref=p_ref.at[0, :, pl.ds(0, H * B)],
        dst_ref=halo_right,
        send_sem=halo_send.at[1],
        recv_sem=halo_recv.at[1],
        device_id=before,
        device_id_type=MESH,
    )
    to_after.start()
    to_before.start()
    pl.loop(Q_BEFORE, FB // GROUP)(form_q)
    to_after.wait()
    to_before.wait()
    pl.semaphore_wait(ready, SIDE - 1)
    has_left = jnp.where(col > 0, 1.0, 0.0).astype(F32)
    has_right = jnp.where(col < N_COL - 1, 1.0, 0.0).astype(F32)
    fill_table(
        table, 0, H // 2, lambda m: halo_left[:, m * W : (m + 1) * W].astype(F32) * has_left
    )
    fill_table(
        table, H + FB, H // 2, lambda m: halo_right[:, m * W : (m + 1) * W].astype(F32) * has_right
    )

    zero = jnp.zeros((B, W), BF16)

    def peer_of(n):
        dz = (2 + n // SIDE) % SIDE
        dx = (2 + n % SIDE) % SIDE
        return ((z + dz) % SIDE) * SIDE + (x + dx) % SIDE

    def source_of(n):
        dz = (2 + n // SIDE) % SIDE
        dx = (2 + n % SIDE) % SIDE
        return ((z + SIDE - dz) % SIDE) * SIDE + (x + SIDE - dx) % SIDE

    def send_copy(chunk, n):
        first, last = CHUNK_TILES[chunk], CHUNK_TILES[chunk + 1]
        part = pl.ds(first * 16, (last - first) * 16)
        peer = peer_of(n)
        return pltpu.make_async_remote_copy(
            src_ref=outgoing.at[peer, part],
            dst_ref=arrived.at[col, part],
            send_sem=sends.at[chunk, n],
            recv_sem=recvs.at[chunk, n],
            device_id=(row, peer),
            device_id_type=MESH,
        )

    def recv_copy(chunk, n):
        first, last = CHUNK_TILES[chunk], CHUNK_TILES[chunk + 1]
        part = pl.ds(first * 16, (last - first) * 16)
        peer = source_of(n)
        return pltpu.make_async_remote_copy(
            src_ref=outgoing.at[peer, part],
            dst_ref=arrived.at[peer, part],
            send_sem=sends.at[chunk, n],
            recv_sem=recvs.at[chunk, n],
            device_id=(row, peer),
            device_id_type=MESH,
        )

    place = (iota((16, WW), 0) * 16 + iota((16, WW), 1) % 16) % CAP

    def list_terms(n):
        p = peer_of(n)
        tags = jnp.full((16, WW), NONE, jnp.int32)
        for j in range(CAP):
            e = items[j, 0, p]
            i = e // KA
            k = e - i * KA
            kp = k // 2
            odd = (k - 2 * kp) == 1
            tile = q_buf[i * KP + kp]
            t = table[cols[k, 0, i]]
            rhs = jnp.concatenate([jnp.where(odd, zero, t), jnp.where(odd, t, zero)], axis=0)
            g = jnp.dot(tile, rhs, preferred_element_type=F32)
            stage[pl.ds(j, 2 * RR, stride=CAP), :] = packed(g)
            slot = jnp.where(j < counts[0, p], slot_scalars[0, e], NONE)
            tags = jnp.where(place == j, slot, tags)
        outgoing[p, pl.ds(0, 16)] = tags.astype(F32).astype(BF16)
        outgoing[p, pl.ds(16, RR * CAP)] = side_by_side(
            stage[: RR * CAP, :], stage[RR * CAP : 2 * RR * CAP, :]
        ).astype(BF16)
        send_copy(0, n).start()

    pl.loop(0, 10)(list_terms)
    pl.loop(11, N_COL)(list_terms)
    for chunk in range(1, CHUNKS):
        for span in ((0, 10), (11, N_COL)):

            @pl.loop(*span)
            def _(n):
                send_copy(chunk, n).start()

    def own_terms(i, here, there):
        rows = pl.ds(pl.multiple_of(((i + FB - 1) % FB) * KS, KS), KS)
        for kp in range(KP):
            tile = q_buf[i * KP + kp]
            t0 = table[cols[2 * kp, 0, i]]
            if 2 * kp + 1 < KA:
                t1 = table[cols[2 * kp + 1, 0, i]]
                rhs = jnp.concatenate(
                    [jnp.concatenate([t0, zero], axis=1), jnp.concatenate([zero, t1], axis=1)],
                    axis=0,
                )
            else:
                rhs = jnp.concatenate([t0, zero], axis=0)
            g = jnp.dot(tile, rhs, preferred_element_type=F32)
            here[pl.ds(2 * kp, 2 * RR, stride=MS), :] = packed(g[:, :W])
            if 2 * kp + 1 < KA:
                here[pl.ds(2 * kp + 1, 2 * RR, stride=MS), :] = packed(g[:, W:])
            for r in range(2 * RR * kp // KP, 2 * RR * (kp + 1) // KP):
                terms[r, rows, :] = there[r * MS : r * MS + KS, :].astype(BF16)

    @pl.loop(0, FB // 2)
    def _(m):
        own_terms(2 * m, mixed, mixed_next)
        own_terms(2 * m + 1, mixed_next, mixed)

    for r in range(2 * RR):
        terms[r, (FB - 1) * KS : FB * KS, :] = mixed_next[r * MS : r * MS + KS, :].astype(BF16)

    def own_sum(chunk):
        for r in range(chunk * PER, (chunk + 1) * PER):
            total = jnp.dot(
                own_hot[...], side_by_side(terms[r], terms[RR + r]), preferred_element_type=F32
            )
            acc[r * SP : (r + 1) * SP, :] += total[:, :W]
            acc[(RR + r) * SP : (RR + r + 1) * SP, :] += total[:, W:]

    acc[...] = jnp.zeros_like(acc)

    lane = iota((1, WW), 1)

    def y_copy(chunk):
        part = pl.ds(chunk * Y_ROWS, Y_ROWS)
        return pltpu.make_async_remote_copy(
            src_ref=y_out.at[part],
            dst_ref=y_in.at[part],
            send_sem=y_send.at[chunk],
            recv_sem=y_recv.at[chunk],
            device_id=partner,
            device_id_type=MESH,
        )

    def merge(chunk):
        for span in ((0, 10), (11, N_COL)):

            @pl.loop(*span)
            def _(n):
                recv_copy(chunk, n).wait_recv()

        if chunk == 0:
            group = iota((16, WW), 1) // 16
            rows = jnp.full((16, WW), float(NONE), F32)
            for src in range(N_COL):
                tags = arrived[src, 0:16, :].astype(F32)
                mine = jnp.logical_and(group == src, src != col)
                rows = jnp.where(mine, tags, rows)
            slot_rows[...] = rows
        for tile in range(CHUNK_TILES[chunk], CHUNK_TILES[chunk + 1]):
            if tile == 0:
                continue
            tau = tile - 1
            first = tau * 16 // CAP
            last = (tau * 16 + 15) // CAP
            slots = slot_rows[tau % CAP : tau % CAP + 1, :]
            r_of = (tau * 16 + lane % 16) // CAP
            values = arrived[:, tile * 16 : tile * 16 + 16, :].reshape(WW, WW)
            sub = iota((SP, WW), 0).astype(F32)
            hot = [
                jnp.where(jnp.where(r_of == r, slots, -1.0) == sub, 1.0, 0.0).astype(BF16)
                for r in range(first, last + 1)
            ]
            more = jnp.dot(jnp.concatenate(hot, axis=0), values, preferred_element_type=F32)
            acc[first * SP : (last + 1) * SP, :] += more[:, :W]
            acc[(RR + first) * SP : (RR + last + 1) * SP, :] += more[:, W:]
        for h in range(2):
            for n in range(PER):
                at = (h * RR + chunk * PER + n) * SP
                y_stage[(h * PER + n) * CS : (h * PER + n + 1) * CS, :] = acc[at : at + CS, :]
        y_out[chunk * Y_ROWS : (chunk + 1) * Y_ROWS, :] = y_stage[...].astype(BF16)
        y_copy(chunk).start()

    weight = keep[row].astype(F32)

    def finish(chunk):
        y_copy(chunk).wait_recv()
        y_stage[...] = y_in[chunk * Y_ROWS : (chunk + 1) * Y_ROWS, :].astype(F32)
        for h in range(2):
            for n in range(PER):
                at = (h * RR + chunk * PER + n) * SP
                more = y_stage[(h * PER + n) * CS : (h * PER + n + 1) * CS, :]
                acc[at : at + CS, :] = (acc[at : at + CS, :] + more) * weight
        low = iota((PER, W), 1) < B
        at = chunk * PER
        for m in range(CS // 2):
            lanes = slice(m * W, (m + 1) * W)
            for half in range(2):
                up = half * RR + at
                a = acc[pl.ds(up * SP + 2 * m, PER, stride=SP), :]
                b = acc[pl.ds(up * SP + 2 * m + 1, PER, stride=SP), :]
                out_ref[0, up : up + PER, lanes] = jnp.where(low, a, pltpu.roll(b, B, 1))
                up = 2 * RR + up
                out_ref[0, up : up + PER, lanes] = jnp.where(low, pltpu.roll(a, B, 1), b)

    def out_copy(n):
        part = pl.ds(n * 8, 8)
        return pltpu.make_async_copy(
            out_ref.at[0, part], out_any.at[0, part], out_sems.at[n]
        )

    for chunk in range(CHUNKS):
        own_sum(chunk)
        merge(chunk)
    for chunk in range(CHUNKS):
        finish(chunk)
        if chunk == 1:
            for n in range(0, 8, 2):
                out_copy(n).start()
    for n in range(1, 8, 2):
        out_copy(n).start()
    for n in range(8):
        out_copy(n).wait()
    for chunk in range(CHUNKS):
        y_copy(chunk).wait_send()
        for span in ((0, 10), (11, N_COL)):

            @pl.loop(*span)
            def _(n):
                send_copy(chunk, n).wait_send()


def on_device(
    a_blocks, a_cols, p_blocks, contrib_peer, contrib_slot, outbound_term_lists, send_count, keep
):
    dma = pltpu.SemaphoreType.DMA
    return pl.pallas_call(
        kernel,
        in_specs=[pl.BlockSpec(memory_space=pl.ANY)] * 8,
        out_specs=pl.BlockSpec(memory_space=pl.ANY),
        out_shape=jax.ShapeDtypeStruct((1, B, CS * B), F32),
        scratch_shapes=[
            pltpu.VMEM((1, B, CS * B), F32),
            pltpu.SMEM((KA, 1, FB), jnp.int32),
            pltpu.SMEM((CAP, 1, N_COL), jnp.int32),
            pltpu.SMEM(send_count.shape, jnp.int32),
            pltpu.SMEM(contrib_slot.shape, jnp.int32),
            pltpu.SMEM(keep.shape, jnp.int32),
            pltpu.VMEM(contrib_slot.shape, jnp.int32),
            pltpu.VMEM(contrib_peer.shape, jnp.int32),
            pltpu.VMEM(p_blocks.shape, BF16),
            pltpu.VMEM((FB, B, KA * B), BF16),
            pltpu.VMEM((FB * KP, B, W), BF16),
            pltpu.VMEM((FB + 2 * H, B, W), BF16),
            pltpu.VMEM((B, H * B), BF16),
            pltpu.VMEM((B, H * B), BF16),
            pltpu.VMEM((2 * RR * CAP + 16, W), F32),
            pltpu.VMEM((N_COL, SEND_ROWS, WW), BF16),
            pltpu.VMEM((N_COL, SEND_ROWS, WW), BF16),
            pltpu.VMEM((2 * RR * MS + KS, W), F32),
            pltpu.VMEM((2 * RR * MS + KS, W), F32),
            pltpu.VMEM((2 * RR, TERMS, W), BF16),
            pltpu.VMEM((2 * RR * SP + SP, W), F32),
            pltpu.VMEM((SP, TERMS), BF16),
            pltpu.VMEM((16, WW), F32),
            pltpu.VMEM((2 * PER * CS, W), F32),
            pltpu.VMEM((CHUNKS * Y_ROWS, W), BF16),
            pltpu.VMEM((CHUNKS * Y_ROWS, W), BF16),
            dma((FB // GROUP,)),
            dma((2,)),
            dma((2,)),
            dma((CHUNKS, N_COL)),
            dma((CHUNKS, N_COL)),
            dma((CHUNKS,)),
            dma((CHUNKS,)),
            pltpu.SemaphoreType.REGULAR,
            dma((8,)),
            dma((8,)),
        ],
        compiler_params=pltpu.CompilerParams(
            collective_id=0, has_side_effects=True, vmem_limit_bytes=62 * 2**20
        ),
        name="galerkin",
    )(
        jnp.transpose(a_cols, (2, 0, 1)),
        jnp.transpose(outbound_term_lists, (2, 0, 1)),
        send_count,
        contrib_slot,
        keep,
        contrib_peer,
        p_blocks,
        a_blocks,
    )


def solution(mesh):
    placed = (
        P("row", "col", None, None),
        P("row", "col", None),
        P("row", None, "col"),
        P("row", "col"),
        P("row", "col"),
        P("row", "col", None),
        P("row", "col"),
        P(),
    )
    return jax.shard_map(
        on_device, mesh=mesh, in_specs=placed, out_specs=P("row", None, "col"), check_vma=False
    )
```
